128 devices in a mesh: dp: 16 (over z, x), seq: 8 (over y, core).
Axes of the slice: x: 4, y: 4, z: 4, core: 2. Of those that a mesh axis runs over, the one named last changes fastest.
Arguments:
- inputs: float32 [128, 160, 768], P(('dp', 'seq')), may hold values from -6 to 6
- lengths: int32 [128], P(('dp', 'seq')), may hold values from 96 to 160, as said below
- w_query: bfloat16 [2, 768, 768], replicated, may hold values from -0.21875 to 0.21875
- b_query: bfloat16 [2, 768], replicated, may hold values from -4 to 4
- w_key: bfloat16 [2, 768, 768], replicated, may hold values from -0.21875 to 0.21875
- w_value: bfloat16 [2, 768, 768], replicated, may hold values from -0.21875 to 0.21875
- b_value: bfloat16 [2, 768], replicated, may hold values from -4 to 4
- w_attn_out: bfloat16 [2, 768, 768], replicated, may hold values from -0.625 to 0.625
- b_attn_out: bfloat16 [2, 768], replicated, may hold values from -4 to 4
- gain_first: bfloat16 [2, 768], replicated, may hold values from 0.5 to 1.5
- shift_first: bfloat16 [2, 768], replicated, may hold values from -4 to 4
- w_in: bfloat16 [2, 768, 3072], replicated, may hold values from -0.21875 to 0.21875
- b_in: bfloat16 [2, 3072], replicated, may hold values from -4 to 4
- w_out: bfloat16 [2, 3072, 768], replicated, may hold values from -0.109375 to 0.109375
- b_out: bfloat16 [2, 768], replicated, may hold values from -4 to 4
- gain_second: bfloat16 [2, 768], replicated, may hold values from 0.5 to 1.5
- shift_second: bfloat16 [2, 768], replicated, may hold values from -4 to 4
- cotangent: float32 [128, 160, 768], P(('dp', 'seq')), may hold values from -24 to 24
Outputs:
- outputs: float32 [128, 160, 768], P(('dp', 'seq'))
- input_grad: float32 [128, 160, 768], P(('dp', 'seq'))
- grad_w_query: float32 [2, 768, 768], P(None, ('dp', 'seq'))
- grad_b_query: float32 [2, 768], P(None, ('dp', 'seq'))
- grad_w_key: float32 [2, 768, 768], P(None, ('dp', 'seq'))
- grad_w_value: float32 [2, 768, 768], P(None, ('dp', 'seq'))
- grad_b_value: float32 [2, 768], P(None, ('dp', 'seq'))
- grad_w_attn_out: float32 [2, 768, 768], P(None, ('dp', 'seq'))
- grad_b_attn_out: float32 [2, 768], P(None, ('dp', 'seq'))
- grad_gain_first: float32 [2, 768], P(None, ('dp', 'seq'))
- grad_shift_first: float32 [2, 768], P(None, ('dp', 'seq'))
- grad_w_in: float32 [2, 768, 3072], P(None, ('dp', 'seq'))
- grad_b_in: float32 [2, 3072], P(None, ('dp', 'seq'))
- grad_w_out: float32 [2, 3072, 768], P(None, ('dp', 'seq'))
- grad_b_out: float32 [2, 768], P(None, ('dp', 'seq'))
- grad_gain_second: float32 [2, 768], P(None, ('dp', 'seq'))
- grad_shift_second: float32 [2, 768], P(None, ('dp', 'seq'))
The draws below stay inside these ranges and needn't reach their ends.
Inputs may be any that keep to these rules, and one draw needn't show every extreme that they name: The lengths of all 128 chains sum to 16384. Chain c holds real tokens at its first lengths[c] positions and padding after them.
All inputs are finite; a program needn't handle non-finite values.
Results may differ from the reference program's by a relative error of at most 0.038.
Values may be sent and summed in bfloat16 or wider, within the bound.
No kernel may reach another device: no remote copies, remote signals or barrier semaphores. Data moves between devices by JAX's collectives and lax.ppermute only.
A program may use at most 256 MiB of HBM per device.

```python
import jax
import jax.numpy as jnp
from jax import lax

D = 768
H = 12
HD = 64
FF = 3072
LAYERS = 2
L = 160
TYPICAL = 128
CHAINS = 128


def draw_lengths(key, part):
    key = jax.random.fold_in(key, 11)
    halves = CHAINS // 2
    shortest = 2 * TYPICAL - L
    first_half = jax.random.randint(jax.random.fold_in(key, 1), (halves,), shortest, L + 1, dtype=jnp.int32)
    first_half = first_half.at[0].set(L)
    joined = jnp.concatenate([first_half, 2 * TYPICAL - first_half])
    order = jax.random.permutation(jax.random.fold_in(key, 2), CHAINS)
    return joined[order].astype(jnp.int32)


def raised(values, key, source, target, blocks, factor):
    def block_of(dim):
        return (jnp.arange(values.shape[dim]) // (values.shape[dim] // blocks)).reshape((-1,) + (1,) * (values.ndim - 1 - dim))

    near = jax.random.permutation(key, blocks)[block_of(target)]
    second = (block_of(target) + blocks // 2) % blocks
    return jnp.where((block_of(source) == near) | (block_of(source) == second), factor * values, values)


def level_of(own_key, extent, shards, smallest, largest):
    level = 1.0
    for position, blocks in shards:
        heights = jax.random.uniform(jax.random.fold_in(jax.random.fold_in(own_key, 6), position), (blocks,), jnp.float32, smallest / len(shards), largest / len(shards))
        level = level * jnp.repeat(jnp.exp(heights), extent[position] // blocks).reshape((-1,) + (1,) * (len(extent) - 1 - position))
    return level


def bell_draw(rng, extent, deviation, most, cuts=(), kind=jnp.bfloat16):
    drawn = jax.random.normal(rng, extent, jnp.float32) * deviation
    if len(cuts) > 0:
        drawn = level_of(rng, extent, cuts, -0.22, 0.18) * drawn
    return jnp.clip(drawn, min=-most, max=most).astype(kind)


def heavy_noise(rng, shape, scale, reach, shards, heavy, held_as=jnp.bfloat16):
    values = scale * jax.random.normal(rng, shape, jnp.float32)
    if shards:
        values = values * level_of(rng, shape, shards, -0.22, 0.18)
    return jnp.clip(raised(values, jax.random.fold_in(rng, 3), *heavy), -reach, reach).astype(held_as)


def setup_inputs(seed: int = 0) -> dict:
    seeds = jax.random.split(jax.random.key(seed), 19)
    return {
        "inputs": bell_draw(seeds[0], (CHAINS, L, D), 1.0, 6.0, ((0, 128),), jnp.float32),
        "lengths": draw_lengths(jax.random.fold_in(seeds[18], 71), 0),
        "w_query": bell_draw(seeds[2], (LAYERS, D, D), D ** -0.5, 0.21875),
        "b_query": bell_draw(seeds[3], (LAYERS, D), 0.3, 4.0),
        "w_key": bell_draw(seeds[4], (LAYERS, D, D), D ** -0.5, 0.21875),
        "w_value": bell_draw(seeds[5], (LAYERS, D, D), D ** -0.5, 0.21875),
        "b_value": bell_draw(seeds[6], (LAYERS, D), 0.3, 4.0),
        "w_attn_out": bell_draw(seeds[7], (LAYERS, D, D), (D // 8) ** -0.5, 0.625),
        "b_attn_out": bell_draw(seeds[8], (LAYERS, D), 0.3, 4.0),
        "gain_first": jnp.clip(1.0 + 0.1 * jax.random.normal(seeds[9], (LAYERS, D), jnp.float32), 0.5, 1.5).astype(jnp.bfloat16),
        "shift_first": bell_draw(seeds[10], (LAYERS, D), 0.3, 4.0),
        "w_in": bell_draw(seeds[11], (LAYERS, D, FF), D ** -0.5, 0.21875),
        "b_in": bell_draw(seeds[12], (LAYERS, FF), 0.3, 4.0),
        "w_out": bell_draw(seeds[13], (LAYERS, FF, D), FF ** -0.5, 0.109375),
        "b_out": bell_draw(seeds[14], (LAYERS, D), 0.3, 4.0),
        "gain_second": jnp.clip(1.0 + 0.1 * jax.random.normal(seeds[15], (LAYERS, D), jnp.float32), 0.5, 1.5).astype(jnp.bfloat16),
        "shift_second": bell_draw(seeds[16], (LAYERS, D), 0.3, 4.0),
        "cotangent": heavy_noise(seeds[17], (CHAINS, L, D), 1.0, 24.0, ((0, 128),), (0, 2, 128, 5.5), jnp.float32),
    }


@jax.custom_vjp
def low(v):
    return lax.optimization_barrier(v.astype(jnp.bfloat16)).astype(jnp.float32)

@jax.custom_vjp
def low_back(v):
    return v

def low_keep(v):
    return (low(v), None)

def low_pass(kept, grad):
    return (grad,)

def back_keep(v):
    return (v, None)

def back_low(kept, grad):
    return (low(grad),)
low.defvjp(low_keep, low_pass)
low_back.defvjp(back_keep, back_low)
EPSILON = 1e-12
HIGHEST = lax.Precision.HIGHEST

def norm_rows(values, gain, shift):
    centre = values - lax.optimization_barrier(jnp.mean(values, axis=-1, keepdims=True))
    spread = lax.optimization_barrier(jnp.mean(centre * centre, axis=-1, keepdims=True))
    return centre * lax.rsqrt(spread + EPSILON) * gain + shift

def linear(left, right):
    return jnp.dot(left, right, precision=HIGHEST)

def encoder_layer(current, live, params):
    w_query, b_query, w_key, w_value, b_value, w_attn_out, b_attn_out, gain_first, shift_first, w_in, b_in, w_out, b_out, gain_second, shift_second = params
    groups = current.shape[0]
    scale = HD ** (-0.5)
    rounded = low(current)
    query = low(low_back(linear(rounded, w_query) + b_query)).reshape(groups, L, H, HD)
    key_heads = low(low_back(linear(rounded, w_key))).reshape(groups, L, H, HD)
    value_heads = low(low_back(linear(rounded, w_value) + b_value)).reshape(groups, L, H, HD)
    raw_scores = jnp.einsum('glhe,gmhe->ghlm', query, key_heads, precision=HIGHEST) * scale
    scores = jnp.where(live[:, None, None, :] > 0, low_back(raw_scores), -1e+30)
    highest = lax.optimization_barrier(jnp.max(scores, axis=-1, keepdims=True))
    exponent_terms = jnp.exp(scores - highest)
    probs = low(exponent_terms / lax.optimization_barrier(jnp.sum(exponent_terms, axis=-1, keepdims=True)))
    context = jnp.einsum('ghlm,gmhe->glhe', probs, value_heads, precision=HIGHEST).reshape(groups, L, D)
    context = low(low_back(context))
    attended = low_back(linear(context, w_attn_out) + b_attn_out)
    hidden = norm_rows(current + attended, gain_first, shift_first)
    hidden_low = low(low_back(hidden))
    before_gelu = low_back(linear(hidden_low, w_in) + b_in)
    activated = low(jax.nn.gelu(before_gelu, approximate=False))
    branch = low(low_back(linear(activated, w_out) + b_out))
    row_mask = live[:, :, None]
    return row_mask * norm_rows(hidden + row_mask * branch, gain_second, shift_second)

def forward(current, live, weights):
    for depth in range(LAYERS):
        current = encoder_layer(current, live, tuple((w[depth] for w in weights)))
    return current

def reference(inputs, lengths, w_query, b_query, w_key, w_value, b_value, w_attn_out, b_attn_out, gain_first, shift_first, w_in, b_in, w_out, b_out, gain_second, shift_second, cotangent):
    weights = tuple((w.astype(jnp.float32) for w in (w_query, b_query, w_key, w_value, b_value, w_attn_out, b_attn_out, gain_first, shift_first, w_in, b_in, w_out, b_out, gain_second, shift_second)))
    positions = jnp.arange(L, dtype=jnp.int32)
    live = (positions[None, :] < lengths[:, None].astype(jnp.int32)).astype(jnp.float32)
    group = 16 if CHAINS % 16 == 0 else CHAINS
    blocks_count = CHAINS // group
    chain_inputs = inputs.reshape(blocks_count, group, L, D)
    chain_live = live.reshape(blocks_count, group, L)
    chain_cot = cotangent.reshape(blocks_count, group, L, D)

    def block_step(totals, item):
        block_in, block_live, block_cot = item
        result, pull = jax.vjp(lambda values, params: forward(values, block_live, params), block_in, weights)
        grad_in, grad_weights = pull(block_cot)
        return (tuple((a + b for a, b in zip(totals, grad_weights))), (result, grad_in))
    zeros = tuple((jnp.zeros_like(w) for w in weights))
    totals, (results, grads_in) = lax.scan(block_step, zeros, (chain_inputs, chain_live, chain_cot))
    return (results.reshape(CHAINS, L, D), grads_in.reshape(CHAINS, L, D), totals[0], totals[1], totals[2], totals[3], totals[4], totals[5], totals[6], totals[7], totals[8], totals[9], totals[10], totals[11], totals[12], totals[13], totals[14])
```

```python
import jax
import jax.numpy as jnp
import numpy as np
from jax import lax
from jax.sharding import PartitionSpec as P

H = 12
HD = 64
LAYERS = 2
EPSILON = 1e-12
FLOAT = jnp.float32
BRAIN = jnp.bfloat16
AXES = ("dp", "seq")
DEVICES = 128
CHIPS = 64


def flip(index, dim):
    core, y, x, z = index & 1, (index >> 1) & 3, (index >> 3) & 3, (index >> 5) & 3
    other = lambda i: i ^ 1 if dim < 3 else 3 - i
    if dim % 3 == 0:
        x = other(x)
    elif dim % 3 == 1:
        y = other(y)
    else:
        z = other(z)
    return z * 32 + x * 8 + y * 2 + core


def bit_of(chip, dim):
    coordinate = ((chip >> 2) & 3, chip & 3, chip >> 4)[dim % 3]
    return ((coordinate ^ (coordinate >> 1)) >> (dim // 3)) & 1


def dim_at(part, step, core):
    return (part + step + 3 * core) % 6


def slot_base(part, core):
    return [
        sum(bit_of(chip, dim_at(part, step, core)) << (5 - step) for step in range(6))
        for chip in range(CHIPS)
    ]


BASES = np.array([[slot_base(part, core) for core in range(2)] for part in range(3)], np.int32)


def slots_of(part, chip, core):
    base = jnp.asarray(BASES)[part, core]
    return base ^ base[chip]


def cube_send(values, part, step):
    pairs = [(i, flip(i, dim_at(part, step, i & 1))) for i in range(DEVICES)]
    return lax.ppermute(values, AXES, pairs)


def core_swap(values):
    return lax.ppermute(values, AXES, [(i, i ^ 1) for i in range(DEVICES)])


def add_low(left, right):
    return (left.astype(FLOAT) + right.astype(FLOAT)).astype(BRAIN)


def cube_sum(send, keep, part):
    for step in range(6):
        got = cube_send(send, part, step)
        if step == 5:
            return add_low(keep, got)
        half = keep.shape[0] // 2
        keep, send = add_low(keep[:half], got[:half]), add_low(keep[half:], got[half:])


def norm_rows(values, gain, shift):
    centre = values - jnp.mean(values, axis=-1, keepdims=True)
    spread = jnp.mean(centre * centre, axis=-1, keepdims=True)
    return centre * lax.rsqrt(spread + EPSILON) * gain + shift


def project(left, right):
    return jnp.dot(left, right, preferred_element_type=FLOAT)


def weight_grad(left, right):
    return lax.dot_general(left, right, (((0,), (0,)), ((), ())), preferred_element_type=FLOAT)


def input_grad(grads, weight):
    return lax.dot_general(grads, weight, (((1,), (1,)), ((), ())), preferred_element_type=FLOAT)


def gelu_pair(values):
    cdf = 0.5 * (1.0 + lax.erf(values * np.float32(0.5**0.5)))
    density = jnp.exp(-0.5 * values * values) * np.float32((2 * np.pi) ** -0.5)
    return values * cdf, cdf + values * density


def heads(values):
    return values.reshape(-1, H, HD)


def layer_forward(flat_in, live_rows, live_keys, params):
    (wq, bq, wk, wv, bv, wo, bo, g1, s1, w_in, b_in, w_out, b_out, g2, s2) = params
    width = flat_in.shape[1]
    rounded = flat_in.astype(BRAIN)
    query = (project(rounded, wq) + bq.astype(FLOAT)).astype(BRAIN)
    keys = project(rounded, wk).astype(BRAIN)
    values = (project(rounded, wv) + bv.astype(FLOAT)).astype(BRAIN)
    raw = jnp.einsum("lhe,mhe->hlm", heads(query), heads(keys), preferred_element_type=FLOAT)
    scores = jnp.where(live_keys[None, None, :], raw * HD**-0.5, -1e30)
    terms = jnp.exp(scores - jnp.max(scores, axis=-1, keepdims=True))
    probs = terms / jnp.sum(terms, axis=-1, keepdims=True)
    context = jnp.einsum("hlm,mhe->lhe", probs.astype(BRAIN), heads(values), preferred_element_type=FLOAT)
    context = context.reshape(-1, width).astype(BRAIN)
    mixed = flat_in + project(context, wo) + bo.astype(FLOAT)
    hidden = norm_rows(mixed, g1.astype(FLOAT), s1.astype(FLOAT))
    hidden_low = hidden.astype(BRAIN)
    act, slope = gelu_pair(project(hidden_low, w_in) + b_in.astype(FLOAT))
    act = act.astype(BRAIN)
    branch = (project(act, w_out) + b_out.astype(FLOAT)).astype(BRAIN)
    summed = hidden + live_rows * branch.astype(FLOAT)
    result = live_rows * norm_rows(summed, g2.astype(FLOAT), s2.astype(FLOAT))
    return result, (rounded, query, keys, values, probs, context, mixed, hidden_low, slope, act, summed)


def exchange(full, columns, core):
    mine, theirs = [], []
    for array in columns:
        half = array.shape[1] // 2
        mine.append(lax.dynamic_slice_in_dim(array, core * half, half, 1))
        theirs.append(lax.dynamic_slice_in_dim(array, (1 - core) * half, half, 1))
    sent = jnp.concatenate(list(full) + theirs, axis=1)
    got = core_swap(sent)
    at, joined = 0, []
    for array in list(full) + mine:
        joined.append(jnp.concatenate([array, got[:, at : at + array.shape[1]]], axis=0))
        at += array.shape[1]
    return joined


def split_slots(chunks, part, chip, core):
    slots = slots_of(part, chip, core)
    order = jnp.zeros((CHIPS,), jnp.int32).at[slots].set(jnp.arange(CHIPS, dtype=jnp.int32))
    chunks = jnp.take(chunks.astype(BRAIN), order, axis=0)
    return chunks[CHIPS // 2 :], chunks[: CHIPS // 2]


def layer_backward(grad_out, live_rows, params, saved, chip, core):
    (wq, bq, wk, wv, bv, wo, bo, g1, s1, w_in, b_in, w_out, b_out, g2, s2) = params
    rounded, query, keys, values, probs, context, mixed, hidden_low, slope, act, summed = saved
    width = rounded.shape[1]
    pull = jax.vjp(norm_rows, summed, g2.astype(FLOAT), s2.astype(FLOAT))[1]
    grad_summed, grad_g2, grad_s2 = pull(grad_out * live_rows)
    g_branch = (live_rows * grad_summed).astype(BRAIN)
    g_pre = (input_grad(g_branch, w_out) * slope).astype(BRAIN)
    g_hidden = input_grad(g_pre, w_in).astype(BRAIN)
    act_all, g_branch_all = exchange((act,), (g_branch,), core)
    grad_c = weight_grad(act_all, g_branch_all).reshape(CHIPS, 48, 384)
    sum_c = cube_sum(*split_slots(grad_c, 0, chip, core), 0)
    hidden_all, g_pre_all = exchange((hidden_low,), (g_pre,), core)
    grad_b = weight_grad(hidden_all, g_pre_all).reshape(CHIPS, 12, 4, 384)
    sum_b = cube_sum(*split_slots(grad_b.swapaxes(1, 2).reshape(CHIPS, 48, 384), 1, chip, core), 1)
    grad_hidden = grad_summed + g_hidden.astype(FLOAT)
    pull = jax.vjp(norm_rows, mixed, g1.astype(FLOAT), s1.astype(FLOAT))[1]
    grad_mixed, grad_g1, grad_s1 = pull(grad_hidden)
    g_att = grad_mixed.astype(BRAIN)
    g_context = heads(input_grad(g_att, wo).astype(BRAIN))
    g_probs = jnp.einsum("lhe,mhe->hlm", g_context, heads(values), preferred_element_type=FLOAT)
    g_values = jnp.einsum("hlm,lhe->mhe", probs.astype(BRAIN), g_context, preferred_element_type=FLOAT)
    g_values = g_values.astype(BRAIN).reshape(-1, width)
    g_raw = (probs * (g_probs - jnp.sum(probs * g_probs, axis=-1, keepdims=True))).astype(BRAIN)
    g_query = jnp.einsum("hlm,mhe->lhe", g_raw, heads(keys), preferred_element_type=FLOAT) * HD**-0.5
    g_query = g_query.astype(BRAIN).reshape(-1, width)
    g_keys = jnp.einsum("hlm,lhe->mhe", g_raw, heads(query), preferred_element_type=FLOAT) * HD**-0.5
    g_keys = g_keys.astype(BRAIN).reshape(-1, width)
    flow = grad_mixed + input_grad(g_query, wq) + input_grad(g_keys, wk) + input_grad(g_values, wv)
    total = lambda g: jnp.sum(g.astype(FLOAT), axis=0)
    vectors = jnp.stack([total(g_query), total(g_values), total(g_att), grad_g1, grad_s1, total(g_branch), grad_g2, grad_s2])
    vectors = jnp.concatenate([vectors, total(g_pre).reshape(width, 4).T, jnp.zeros((116, width), FLOAT)])
    x_all, ctx_all, gq, gk, gv, ga = exchange((rounded, context), (g_query, g_keys, g_values, g_att), core)
    pieces = [weight_grad(x_all, gq), weight_grad(x_all, gk), weight_grad(x_all, gv), weight_grad(ctx_all, ga), vectors.T]
    pieces = [p.reshape(CHIPS, 12, -1, 128).swapaxes(1, 2).reshape(CHIPS, -1, 128) for p in pieces]
    pieces.append(jnp.zeros((CHIPS, 4, 128), FLOAT))
    grad_a = jnp.concatenate(pieces, axis=1)
    sum_a = cube_sum(*split_slots(grad_a, 2, chip, core), 2)
    return flow, (sum_a[0], sum_b[0], sum_c[0])


def finish(sums, core):
    sum_a, sum_b, sum_c = sums
    rows_a = sum_a[:156].reshape(13, 2, 6, 128)
    rows_b = sum_b.reshape(4, 2, 6, 384)
    rows_c = sum_c.reshape(2, 24, 384)
    mine = [jnp.take(rows_a, core, axis=1), jnp.take(rows_b, core, axis=1), jnp.take(rows_c, core, axis=0)]
    theirs = [jnp.take(rows_a, 1 - core, axis=1), jnp.take(rows_b, 1 - core, axis=1), jnp.take(rows_c, 1 - core, axis=0)]
    got = core_swap(jnp.concatenate([t.reshape(-1, 128) for t in theirs], axis=0))
    got_a = got[:78].reshape(13, 6, 128)
    got_b = got[78 : 78 + 72].reshape(4, 6, 384)
    got_c = got[150:].reshape(24, 384)
    pair = lambda a, b: (jnp.where(core == 0, a, b).astype(FLOAT), jnp.where(core == 0, b, a).astype(FLOAT))
    a0, a1 = pair(mine[0], got_a)
    b0, b1 = pair(mine[1], got_b)
    c0, c1 = pair(mine[2], got_c)
    square = lambda m: jnp.concatenate([a0[3 * m + j] for j in range(3)] + [a1[3 * m + j] for j in range(3)], axis=1)
    vectors = a0[12] + a1[12]
    w_in = jnp.concatenate([b0[k] for k in range(4)] + [b1[k] for k in range(4)], axis=1)
    w_out = jnp.concatenate([c0, c1], axis=1)
    v = [vectors[:, i] for i in range(8)]
    b_in = vectors[:, 8:12].reshape(24)
    return (square(0), v[0], square(1), square(2), v[1], square(3), v[2], v[3], v[4], w_in, b_in, w_out, v[5], v[6], v[7])


def body(inputs, lengths, *weights):
    params_all, cotangent = weights[:-1], weights[-1]
    chains, length, width = inputs.shape
    index = lax.axis_index(AXES)
    chip, core = index // 2, index % 2
    live_keys = jnp.arange(length, dtype=jnp.int32) < lengths[0]
    live_rows = live_keys.reshape(-1, 1).astype(FLOAT)
    current = inputs.reshape(length, width)
    kept = []
    for depth in range(LAYERS):
        current, saved = layer_forward(current, live_rows, live_keys, [p[depth] for p in params_all])
        kept.append(saved)
    flow = cotangent.reshape(length, width)
    outs = [None] * LAYERS
    for depth in reversed(range(LAYERS)):
        flow, sums = layer_backward(flow, live_rows, [p[depth] for p in params_all], kept[depth], chip, core)
        outs[depth] = finish(sums, core)
    stacked = tuple(jnp.stack([outs[d][m] for d in range(LAYERS)]) for m in range(len(params_all)))
    return (current.reshape(inputs.shape), flow.reshape(inputs.shape)) + stacked


def solution(mesh):
    rows = P(AXES, None, None)
    in_specs = (rows, P(AXES)) + (P(),) * 15 + (rows,)
    wide, thin = P(None, AXES, None), P(None, AXES)
    out_specs = (rows, rows, wide, thin, wide, wide, thin, wide, thin, thin, thin, wide, thin, wide, thin, thin, thin)
    return jax.shard_map(body, mesh=mesh, in_specs=in_specs, out_specs=out_specs, check_vma=False)
```

```python
import jax
import jax.numpy as jnp
import numpy as np
from jax import lax
from jax.experimental import pallas as pl
from jax.experimental.pallas import tpu as pltpu
from jax.sharding import PartitionSpec as P

PAIRS = 6
LAYERS = 2
ROWS = 160
D = 768
FF = 3072
HALF = 384
EPSILON = 1e-12
FLOAT = jnp.float32
BRAIN = jnp.bfloat16
AXES = ("dp", "seq")
DEVICES = 128
CHIPS = 64


def flip(index, dim):
    core, y, x, z = index & 1, (index >> 1) & 3, (index >> 3) & 3, (index >> 5) & 3
    other = lambda i: i ^ 1 if dim < 3 else 3 - i
    if dim % 3 == 0:
        x = other(x)
    elif dim % 3 == 1:
        y = other(y)
    else:
        z = other(z)
    return z * 32 + x * 8 + y * 2 + core


def bit_of(chip, dim):
    coordinate = ((chip >> 2) & 3, chip & 3, chip >> 4)[dim % 3]
    return ((coordinate ^ (coordinate >> 1)) >> (dim // 3)) & 1


def dim_at(part, step, core):
    return (part + step + 3 * core) % 6


def slot_base(part, core):
    return [
        sum(bit_of(chip, dim_at(part, step, core)) << (5 - step) for step in range(6))
        for chip in range(CHIPS)
    ]


BASES = np.array([[slot_base(part, core) for core in range(2)] for part in range(3)], np.int32)


def slots_of(part, chip, core):
    base = jnp.asarray(BASES)[part, core]
    return base ^ base[chip]


def cube_send(values, part, step):
    pairs = [(i, flip(i, dim_at(part, step, i & 1))) for i in range(DEVICES)]
    return lax.ppermute(values, AXES, pairs)


def core_swap(values):
    return lax.ppermute(values, AXES, [(i, i ^ 1) for i in range(DEVICES)])


def add_low(left, right):
    return (left.astype(FLOAT) + right.astype(FLOAT)).astype(BRAIN)


def cube_sum(send, keep, part):
    for step in range(6):
        got = cube_send(send, part, step)
        if step == 5:
            return add_low(keep, got)
        half = keep.shape[0] // 2
        keep, send = add_low(keep[:half], got[:half]), add_low(keep[half:], got[half:])


def dot(left, right):
    return lax.dot_general(left, right, (((1,), (0,)), ((), ())), preferred_element_type=FLOAT)


def dot_right(left, right):
    return lax.dot_general(left, right, (((1,), (1,)), ((), ())), preferred_element_type=FLOAT)


def dot_left(left, right):
    return lax.dot_general(left, right, (((0,), (0,)), ((), ())), preferred_element_type=FLOAT)


def centred(values):
    centre = values - jnp.mean(values, axis=-1, keepdims=True)
    inverse = lax.rsqrt(jnp.mean(centre * centre, axis=-1, keepdims=True) + EPSILON)
    return centre * inverse, inverse


def norm_back(grad, normal, inverse, gain):
    scaled = grad * gain
    back = scaled - jnp.mean(scaled, axis=-1, keepdims=True)
    back = back - normal * jnp.mean(scaled * normal, axis=-1, keepdims=True)
    return back * inverse, total(grad * normal), total(grad)


def total(values):
    return jnp.sum(values.astype(FLOAT), axis=0, keepdims=True)


def row(ref, layer):
    return ref[layer : layer + 1, :].astype(FLOAT)


def gelu_pair(values):
    cdf = 0.5 + 0.5 * lax.erf(values * np.float32(0.5**0.5))
    density = jnp.exp(-0.5 * values * values) * np.float32((2 * np.pi) ** -0.5)
    return values * cdf, cdf + values * density


def live_of(length, shape, axis):
    return lax.broadcasted_iota(jnp.int32, shape, axis) < length


def two_heads(pair):
    first = lax.broadcasted_iota(jnp.int32, pair.shape, 1) < 64
    none = jnp.zeros_like(pair)
    return jnp.concatenate([jnp.where(first, pair, none), jnp.where(first, none, pair)], axis=0)


def join_heads(both):
    first = lax.broadcasted_iota(jnp.int32, (ROWS, 128), 1) < 64
    return jnp.where(first, both[:ROWS], both[ROWS:])


def half_of(ref, core, width, at=0):
    return ref[:, pl.ds(pl.multiple_of(at + core * width, 128), width)]


X_ACT, X_HID, X_IN, X_CTX = 0, FF, FF + D, FF + 2 * D
X_WIDTH = FF + 3 * D
G_WIDTH = FF // 2 + HALF


def forward_layer(layer, x, length, small, weights, ready, x_ref, qkv_ref, probs_ref, mixed_ref, slope_ref):
    bq, bv, bo, g1, s1, b_in, b_out, g2, s2 = small
    wq, wk, wv, wo, w_in, w_out = weights
    rounded = x.astype(BRAIN)
    x_ref[:, X_IN : X_IN + D] = rounded
    ready(layer, 0)
    qkv_ref[:, 0:D] = ((dot(rounded, wq[layer]) + row(bq, layer)).astype(BRAIN) * 0.125).astype(BRAIN)
    ready(layer, 1)
    qkv_ref[:, D : 2 * D] = dot(rounded, wk[layer]).astype(BRAIN)
    ready(layer, 2)
    qkv_ref[:, 2 * D : 3 * D] = (dot(rounded, wv[layer]) + row(bv, layer)).astype(BRAIN)
    keys_live = live_of(length, (2 * ROWS, ROWS), 1)
    for pair in range(PAIRS):
        lanes = lambda m: slice(m * D + 128 * pair, m * D + 128 * pair + 128)
        scores = dot_right(two_heads(qkv_ref[:, lanes(0)]), qkv_ref[:, lanes(1)])
        scores = jnp.where(keys_live, scores, -1e30)
        terms = jnp.exp(scores - jnp.max(scores, axis=-1, keepdims=True))
        probs = (terms / jnp.sum(terms, axis=-1, keepdims=True)).astype(BRAIN)
        probs_ref[pair] = probs
        context = join_heads(dot(probs, qkv_ref[:, lanes(2)]))
        x_ref[:, X_CTX + 128 * pair : X_CTX + 128 * pair + 128] = context.astype(BRAIN)
    ready(layer, 3)
    mixed = x + dot(x_ref[:, X_CTX : X_CTX + D], wo[layer]) + row(bo, layer)
    mixed_ref[...] = mixed
    hidden = centred(mixed)[0] * row(g1, layer) + row(s1, layer)
    hidden_low = hidden.astype(BRAIN)
    x_ref[:, X_HID : X_HID + D] = hidden_low
    ready(layer, 4)
    for part in range(4):
        at = slice(part * D, part * D + D)
        pre = dot(hidden_low, w_in[layer, :, at]) + b_in[layer : layer + 1, at].astype(FLOAT)
        act, slope = gelu_pair(pre)
        x_ref[:, at] = act.astype(BRAIN)
        slope_ref[:, at] = slope.astype(BRAIN)
    ready(layer, 5)
    branch = (dot(x_ref[:, :FF], w_out[layer]) + row(b_out, layer)).astype(BRAIN).astype(FLOAT)
    live = live_of(length, (ROWS, 1), 0)
    summed = hidden + jnp.where(live, branch, 0.0)
    normal, inverse = centred(summed)
    result = jnp.where(live, normal * row(g2, layer) + row(s2, layer), 0.0)
    return result, summed, normal, inverse


def forward_kernel(
    place, x_in, bq, bv, bo, g1, s1, b_in, b_out, g2, s2,
    wq_any, wk_any, wv_any, wo_any, wi_any, wu_any, cotangent,
    out, x0, x1, qkv0, qkv1, probs0, probs1, mixed0, mixed1, summed0, slope0,
    g_mine, g_theirs, grad_hidden, vectors, bias_in,
    wq, wk, wv, wo, wi, wu, slope1, g_pre, g_low, sems,
):
    length, core = place[0], place[1]
    weights = (wq, wk, wv, wo, wi, wu)
    copies = [
        [pltpu.make_async_copy(a.at[layer], w.at[layer], sems.at[layer, n]) for n, (a, w) in enumerate(zip((wq_any, wk_any, wv_any, wo_any, wi_any, wu_any), weights))]
        for layer in range(LAYERS)
    ]
    for layer in range(LAYERS):
        for copy in copies[layer]:
            copy.start()
    ready = lambda layer, n: copies[layer][n].wait()
    small = (bq, bv, bo, g1, s1, b_in, b_out, g2, s2)
    middle, summed, _, _ = forward_layer(0, x_in[...], length, small, weights, ready, x0, qkv0, probs0, mixed0, slope0)
    summed0[...] = summed
    result, _, normal, inverse = forward_layer(1, middle, length, small, weights, ready, x1, qkv1, probs1, mixed1, slope1)
    out[...] = result
    feed_back(1, cotangent[...], length, core, normal, inverse, g2, wi.at[1], wu.at[1], slope1, g_pre, g_low,
              g_mine, g_theirs, grad_hidden, vectors, bias_in)


def feed_back(layer, grad_out, length, core, normal, inverse, g2, wi, wu, slope, g_pre, g_low,
              g_mine, g_theirs, grad_hidden, vectors, bias_in):
    live = live_of(length, (ROWS, 1), 0)
    grad_live = jnp.where(live, grad_out, 0.0)
    grad_summed, grad_gain, grad_shift = norm_back(grad_live, normal, inverse, row(g2, layer))
    low = jnp.where(live, grad_summed, 0.0).astype(BRAIN)
    g_low[...] = low
    vectors[...] = jnp.concatenate([total(low), grad_gain, grad_shift, jnp.zeros((5, D), FLOAT)], axis=0)
    for part in range(4):
        at = slice(part * D, part * D + D)
        grads = (dot_right(low, wu[at, :]) * slope[:, at].astype(FLOAT)).astype(BRAIN)
        g_pre[:, at] = grads
        bias_in[:, at] = total(grads)
    grad_hidden[...] = grad_summed + dot_right(g_pre[...], wi[...]).astype(BRAIN).astype(FLOAT)
    g_mine[:, : FF // 2] = half_of(g_pre, core, FF // 2)
    g_mine[:, FF // 2 :] = half_of(g_low, core, HALF)
    g_theirs[:, : FF // 2] = half_of(g_pre, 1 - core, FF // 2)
    g_theirs[:, FF // 2 :] = half_of(g_low, 1 - core, HALF)


def feed_kernel(place, grad_out, summed, g2, slope, wi_any, wu_any,
                g_mine, g_theirs, grad_hidden, vectors, bias_in, wi, wu, g_pre, g_low, sems):
    copies = [pltpu.make_async_copy(wu_any.at[0], wu, sems.at[0]), pltpu.make_async_copy(wi_any.at[0], wi, sems.at[1])]
    for copy in copies:
        copy.start()
    normal, inverse = centred(summed[...])
    for copy in copies:
        copy.wait()
    feed_back(0, grad_out[...], place[0], place[1], normal, inverse, g2, wi, wu, slope, g_pre, g_low,
              g_mine, g_theirs, grad_hidden, vectors, bias_in)


def attend_kernel(layer, place, grad_hidden, mixed, g1, x_in, qkv, probs, wq_any, wk_any, wv_any, wo_any,
                  flow, g_mine, g_theirs, vectors, wq, wk, wv, wo, g_all, g_context, sems):
    core = place[1]
    copies = [pltpu.make_async_copy(a.at[layer], w, sems.at[n]) for n, (a, w) in enumerate(((wo_any, wo), (wq_any, wq), (wk_any, wk), (wv_any, wv)))]
    for copy in copies:
        copy.start()
    normal, inverse = centred(mixed[...])
    grad_mixed, grad_gain, grad_shift = norm_back(grad_hidden[...], normal, inverse, row(g1, layer))
    low = grad_mixed.astype(BRAIN)
    g_all[:, 3 * D :] = low
    copies[0].wait()
    g_context[...] = dot_right(low, wo[...]).astype(BRAIN)
    for pair in range(PAIRS):
        lanes = lambda m: slice(m * D + 128 * pair, m * D + 128 * pair + 128)
        context_two = two_heads(g_context[:, lanes(0)])
        probs_two = probs[pair]
        g_probs = dot_right(context_two, qkv[:, lanes(2)])
        g_all[:, lanes(2)] = dot_left(probs_two, context_two).astype(BRAIN)
        weighted = probs_two.astype(FLOAT)
        g_raw = weighted * (g_probs - jnp.sum(weighted * g_probs, axis=-1, keepdims=True))
        g_raw = g_raw.astype(BRAIN)
        g_all[:, lanes(0)] = (join_heads(dot(g_raw, qkv[:, lanes(1)])) * 0.125).astype(BRAIN)
        g_all[:, lanes(1)] = dot_left(g_raw, two_heads(qkv[:, lanes(0)])).astype(BRAIN)
    for copy in copies[1:]:
        copy.wait()
    flow[...] = (
        grad_mixed
        + dot_right(g_all[:, :D], wq[...])
        + dot_right(g_all[:, D : 2 * D], wk[...])
        + dot_right(g_all[:, 2 * D : 3 * D], wv[...])
    )
    vectors[...] = jnp.concatenate(
        [total(g_all[:, :D]), total(g_all[:, 2 * D : 3 * D]), total(low), grad_gain, grad_shift, jnp.zeros((3, D), FLOAT)], axis=0
    )
    for m in range(4):
        g_mine[:, m * HALF : m * HALF + HALF] = half_of(g_all, core, HALF, m * D)
        g_theirs[:, m * HALF : m * HALF + HALF] = half_of(g_all, 1 - core, HALF, m * D)


def put(out_send, out_keep, slot, chunk):
    @pl.when(slot >= CHIPS // 2)
    def _():
        out_send[slot - CHIPS // 2] = chunk

    @pl.when(slot < CHIPS // 2)
    def _():
        out_keep[slot] = chunk


def grad_out_kernel(slots, x_own, x_got, g_own, g_got, send, keep):
    for piece in range(8):
        at = slice(piece * 384, piece * 384 + 384)
        grads = dot_left(x_own[:, at], g_own[...]) + dot_left(x_got[:, at], g_got[...])
        grads = grads.astype(BRAIN)
        for n in range(8):
            put(send, keep, slots[piece * 8 + n], grads[48 * n : 48 * n + 48])


def grad_in_kernel(slots, x_own, x_got, g_own, g_got, send, keep):
    for piece in range(2):
        at = slice(piece * 384, piece * 384 + 384)
        blocks = []
        for k in range(4):
            cols = slice(k * 384, k * 384 + 384)
            blocks.append(dot_left(x_own[:, at], g_own[:, cols]) + dot_left(x_got[:, at], g_got[:, cols]))
        for n in range(32):
            chunk = jnp.concatenate([b[12 * n : 12 * n + 12] for b in blocks], axis=0)
            put(send, keep, slots[piece * 32 + n], chunk.astype(BRAIN))


def grad_att_kernel(slots, x_own, c_own, x_got, c_got, g_own, g_got, vec_a, vec_f, vec_b, send, keep):
    vectors = jnp.concatenate([vec_a[0:5], vec_f[0:3], vec_b[0:4], jnp.zeros((116, D), FLOAT)], axis=0).T
    for piece in range(2):
        at = slice(piece * 384, piece * 384 + 384)
        blocks = []
        for m in range(4):
            cols = slice(m * 384, m * 384 + 384)
            own, got = (x_own, x_got) if m < 3 else (c_own, c_got)
            blocks.append(dot_left(own[:, at], g_own[:, cols]) + dot_left(got[:, at], g_got[:, cols]))
        blocks = [b[:, 128 * j : 128 * j + 128] for b in blocks for j in range(3)] + [vectors[at]]
        for n in range(32):
            chunk = jnp.concatenate([b[12 * n : 12 * n + 12] for b in blocks] + [jnp.zeros((4, 128), FLOAT)], axis=0)
            put(send, keep, slots[piece * 32 + n], chunk.astype(BRAIN))


def shape(*dims, kind=BRAIN):
    return jax.ShapeDtypeStruct(dims, kind)


VMEM = pl.BlockSpec(memory_space=pltpu.VMEM)
SMEM = pl.BlockSpec(memory_space=pltpu.SMEM)
ANY = pl.BlockSpec(memory_space=pl.ANY)


def call(kernel, ins, outs, scratch, args, flops, limit=60):
    return pl.pallas_call(
        kernel,
        in_specs=ins,
        out_specs=[VMEM] * len(outs),
        out_shape=outs,
        scratch_shapes=scratch,
        compiler_params=pltpu.CompilerParams(vmem_limit_bytes=limit * 2**20),
        cost_estimate=pl.CostEstimate(flops=flops, bytes_accessed=2**23, transcendentals=0),
    )(*args)


def columns(width, index):
    return pl.BlockSpec((ROWS, width), lambda i: (0, index))


def weight_call(kernel, specs, args, chunk, slots):
    half = CHIPS // 2
    return pl.pallas_call(
        kernel,
        grid=(1,),
        in_specs=[SMEM] + specs,
        out_specs=[VMEM, VMEM],
        out_shape=[shape(half, *chunk), shape(half, *chunk)],
        compiler_params=pltpu.CompilerParams(vmem_limit_bytes=40 * 2**20),
        cost_estimate=pl.CostEstimate(flops=2 * 320 * D * D * 2, bytes_accessed=2**23, transcendentals=0),
    )(slots, *args)


def finish(sums, core):
    sum_a, sum_b, sum_c = sums
    rows_a = sum_a[:156].reshape(13, 2, 6, 128)
    rows_b = sum_b.reshape(4, 2, 6, 384)
    rows_c = sum_c.reshape(2, 24, 384)
    mine = [jnp.take(rows_a, core, axis=1), jnp.take(rows_b, core, axis=1), jnp.take(rows_c, core, axis=0)]
    theirs = [jnp.take(rows_a, 1 - core, axis=1), jnp.take(rows_b, 1 - core, axis=1), jnp.take(rows_c, 1 - core, axis=0)]
    got = core_swap(jnp.concatenate([t.reshape(-1, 128) for t in theirs], axis=0))
    got_a = got[:78].reshape(13, 6, 128)
    got_b = got[78 : 78 + 72].reshape(4, 6, 384)
    got_c = got[150:].reshape(24, 384)
    pair = lambda a, b: (jnp.where(core == 0, a, b).astype(FLOAT), jnp.where(core == 0, b, a).astype(FLOAT))
    a0, a1 = pair(mine[0], got_a)
    b0, b1 = pair(mine[1], got_b)
    c0, c1 = pair(mine[2], got_c)
    square = lambda m: jnp.concatenate([a0[3 * m + j] for j in range(3)] + [a1[3 * m + j] for j in range(3)], axis=1)
    vectors = a0[12] + a1[12]
    w_in = jnp.concatenate([b0[k] for k in range(4)] + [b1[k] for k in range(4)], axis=1)
    w_out = jnp.concatenate([c0, c1], axis=1)
    v = [vectors[:, i] for i in range(8)]
    b_in = vectors[:, 8:12].reshape(24)
    return (square(0), v[0], square(1), square(2), v[1], square(3), v[2], v[3], v[4], w_in, b_in, w_out, v[5], v[6], v[7])


def body(inputs, lengths, wq, bq, wk, wv, bv, wo, bo, g1, s1, w_in, b_in, w_out, b_out, g2, s2, cotangent):
    index = lax.axis_index(AXES)
    chip, core = index // 2, index % 2
    place = jnp.stack([lengths[0], core]).astype(jnp.int32)
    wide = shape(ROWS, D, kind=FLOAT)
    x_shape, qkv, probs = shape(ROWS, X_WIDTH), shape(ROWS, 3 * D), shape(PAIRS, 2 * ROWS, ROWS)
    back_shapes = [shape(ROWS, G_WIDTH), shape(ROWS, G_WIDTH), wide, shape(8, D, kind=FLOAT), shape(1, FF, kind=FLOAT)]
    squares = [pltpu.VMEM((LAYERS, D, D), BRAIN)] * 4
    first = call(
        forward_kernel,
        [SMEM] + [VMEM] * 10 + [ANY] * 6 + [VMEM],
        [wide, x_shape, x_shape, qkv, qkv, probs, probs, wide, wide, wide, shape(ROWS, FF)] + back_shapes,
        squares
        + [pltpu.VMEM((LAYERS, D, FF), BRAIN), pltpu.VMEM((LAYERS, FF, D), BRAIN)]
        + [pltpu.VMEM((ROWS, FF), BRAIN), pltpu.VMEM((ROWS, FF), BRAIN), pltpu.VMEM((ROWS, D), BRAIN)]
        + [pltpu.SemaphoreType.DMA((LAYERS, 6))],
        (place, inputs.reshape(ROWS, D), bq, bv, bo, g1, s1, b_in, b_out, g2, s2, wq, wk, wv, wo, w_in, w_out, cotangent.reshape(ROWS, D)),
        10**10,
    )
    out, x0, x1, qkv0, qkv1, probs0, probs1, mixed0, mixed1, summed0, slope0 = first[:11]
    feeds = [None, first[11:]]
    xs, qkvs, probses, mixeds = (x0, x1), (qkv0, qkv1), (probs0, probs1), (mixed0, mixed1)
    flow = None
    layers = [None] * LAYERS
    for layer in (1, 0):
        if layer == 0:
            feeds[0] = call(
                feed_kernel,
                [SMEM] + [VMEM] * 4 + [ANY] * 2,
                back_shapes,
                [pltpu.VMEM((D, FF), BRAIN), pltpu.VMEM((FF, D), BRAIN), pltpu.VMEM((ROWS, FF), BRAIN), pltpu.VMEM((ROWS, D), BRAIN)]
                + [pltpu.SemaphoreType.DMA((2,))],
                (place, flow, summed0, g2, slope0, w_in, w_out),
                2 * 10**9,
            )
        g_mine, g_theirs, grad_hidden, vec_f, bias_in = feeds[layer]
        x_own = xs[layer]
        x_got, g_got = core_swap(x_own), core_swap(g_theirs)
        slots = [slots_of(part, chip, core) for part in range(3)]
        send_c, keep_c = weight_call(
            grad_out_kernel, [columns(FF, 0), columns(FF, 0), columns(HALF, 4), columns(HALF, 4)],
            (x_own, x_got, g_mine, g_got), (48, 384), slots[0])
        send_b, keep_b = weight_call(
            grad_in_kernel, [columns(D, 4), columns(D, 4), columns(FF // 2, 0), columns(FF // 2, 0)],
            (x_own, x_got, g_mine, g_got), (48, 384), slots[1])
        flow, a_mine, a_theirs, vec_a = call(
            lambda *refs, layer=layer: attend_kernel(layer, *refs),
            [SMEM] + [VMEM] * 3 + [VMEM] * 3 + [ANY] * 4,
            [wide, shape(ROWS, 4 * HALF), shape(ROWS, 4 * HALF), shape(8, D, kind=FLOAT)],
            [pltpu.VMEM((D, D), BRAIN)] * 4 + [pltpu.VMEM((ROWS, 4 * D), BRAIN), pltpu.VMEM((ROWS, D), BRAIN), pltpu.SemaphoreType.DMA((4,))],
            (place, grad_hidden, mixeds[layer], g1, x_own, qkvs[layer], probses[layer], wq, wk, wv, wo),
            10**9,
        )
        a_got = core_swap(a_theirs)
        vec_b = bias_in.reshape(D, 4).T
        send_a, keep_a = weight_call(
            grad_att_kernel,
            [columns(D, 5), columns(D, 6), columns(D, 5), columns(D, 6), VMEM, VMEM, VMEM, VMEM, VMEM],
            (x_own, x_own, x_got, x_got, a_mine, a_got, vec_a, vec_f, vec_b), (160, 128), slots[2])
        sums = (cube_sum(send_a, keep_a, 2)[0], cube_sum(send_b, keep_b, 1)[0], cube_sum(send_c, keep_c, 0)[0])
        layers[layer] = finish(sums, core)
    stacked = tuple(jnp.stack([layers[d][m] for d in range(LAYERS)]) for m in range(15))
    return (out.reshape(inputs.shape), flow.reshape(inputs.shape)) + stacked


def solution(mesh):
    rows = P(AXES, None, None)
    in_specs = (rows, P(AXES)) + (P(),) * 15 + (rows,)
    wide, thin = P(None, AXES, None), P(None, AXES)
    out_specs = (rows, rows, wide, thin, wide, wide, thin, wide, thin, thin, thin, wide, thin, wide, thin, thin, thin)
    return jax.shard_map(body, mesh=mesh, in_specs=in_specs, out_specs=out_specs, check_vma=False)
```

```python
import jax
import jax.numpy as jnp
import numpy as np
from jax import lax
from jax.experimental import pallas as pl
from jax.experimental.pallas import tpu as pltpu
from jax.sharding import PartitionSpec as P

PAIRS = 6
LAYERS = 2
ROWS = 160
D = 768
FF = 3072
HALF = 384
EPSILON = 1e-12
FLOAT = jnp.float32
BRAIN = jnp.bfloat16
AXES = ("dp", "seq")
DEVICES = 128
CHIPS = 64


def flip(index, dim):
    core, y, x, z = index & 1, (index >> 1) & 3, (index >> 3) & 3, (index >> 5) & 3
    other = lambda i: i ^ 1 if dim < 3 else 3 - i
    if dim % 3 == 0:
        x = other(x)
    elif dim % 3 == 1:
        y = other(y)
    else:
        z = other(z)
    return z * 32 + x * 8 + y * 2 + core


def bit_of(chip, dim):
    coordinate = ((chip >> 2) & 3, chip & 3, chip >> 4)[dim % 3]
    return ((coordinate ^ (coordinate >> 1)) >> (dim // 3)) & 1


def dim_at(part, step, core):
    return (part + step) % 3 + 3 * core if step < 3 else step - 3 + 3 * (1 - core)


def slot_base(part, core, chip):
    return sum(bit_of(chip, dim_at(part, step, core)) << (5 - step) for step in range(6))


def own_place():
    index = lax.axis_index(AXES[0]) * 8 + lax.axis_index(AXES[1])
    return index // 2, index % 2


def slots_of(part):
    chip, core = own_place()
    own = jnp.where(core == 0, slot_base(part, 0, chip), slot_base(part, 1, chip))
    return lambda other: jnp.where(core == 0, slot_base(part, 0, other), slot_base(part, 1, other)) ^ own


def cube_send(values, part, step):
    pairs = [(i, flip(i, dim_at(part, step, i & 1))) for i in range(DEVICES)]
    return lax.ppermute(values, AXES, pairs)


def core_swap(values):
    return lax.ppermute(values, AXES, [(i, i ^ 1) for i in range(DEVICES)])


def add_low(left, right):
    return (left.astype(FLOAT) + right.astype(FLOAT)).astype(BRAIN)


def split_sum(keep, got):
    half = keep.shape[0] // 2
    return add_low(keep[:half], got[:half]), add_low(keep[half:], got[half:])


def cube_start(send, keep, part):
    for step in range(3):
        got = cube_send(send, part, step)
        if step == 2:
            return keep, got
        keep, send = split_sum(keep, got)


def cube_end(parts):
    keep, send = merge(*parts)
    for step in range(3, 6):
        got = cube_send(send, 0, step)
        if step == 5:
            return keep, got
        keep, send = split_sum(keep, got)


def dot(left, right):
    return lax.dot_general(left, right, (((1,), (0,)), ((), ())), preferred_element_type=FLOAT)


def dot_right(left, right):
    return lax.dot_general(left, right, (((1,), (1,)), ((), ())), preferred_element_type=FLOAT)


def dot_left(left, right):
    return lax.dot_general(left, right, (((0,), (0,)), ((), ())), preferred_element_type=FLOAT)


def centred(values):
    centre = values - jnp.mean(values, axis=-1, keepdims=True)
    inverse = lax.rsqrt(jnp.mean(centre * centre, axis=-1, keepdims=True) + EPSILON)
    return centre * inverse, inverse


def norm_back(grad, normal, inverse, gain):
    scaled = grad * gain
    back = scaled - jnp.mean(scaled, axis=-1, keepdims=True)
    back = back - normal * jnp.mean(scaled * normal, axis=-1, keepdims=True)
    return back * inverse, total(grad * normal), total(grad)


def total(values):
    return jnp.sum(values.astype(FLOAT), axis=0, keepdims=True)


def row(ref, layer):
    return ref[layer : layer + 1, :].astype(FLOAT)


def gelu_pair(values):
    cdf = 0.5 + 0.5 * lax.erf(values * np.float32(0.5**0.5))
    density = jnp.exp(-0.5 * values * values) * np.float32((2 * np.pi) ** -0.5)
    return values * cdf, cdf + values * density


def live_of(length, shape, axis):
    return lax.broadcasted_iota(jnp.int32, shape, axis) < length


def two_heads(pair):
    first = lax.broadcasted_iota(jnp.int32, pair.shape, 1) < 64
    none = jnp.zeros_like(pair)
    return jnp.concatenate([jnp.where(first, pair, none), jnp.where(first, none, pair)], axis=0)


def join_heads(both):
    first = lax.broadcasted_iota(jnp.int32, (ROWS, 128), 1) < 64
    return jnp.where(first, both[:ROWS], both[ROWS:])


def half_of(ref, core, width, at=0):
    return ref[:, pl.ds(pl.multiple_of(at + core * width, 128), width)]


F_HID, F_PRE, F_LOW = FF, FF + D, FF + D + FF // 2
F_WIDTH = FF + D + FF // 2 + HALF
A_CTX, A_GRAD = D, 2 * D
A_WIDTH = 2 * D + 4 * HALF


class Stream:
    def __init__(self, pairs, sems, ahead):
        self.copies = [pltpu.make_async_copy(source, target, sems.at[n]) for n, (source, target) in enumerate(pairs)]
        self.ahead, self.done, self.begun = ahead, 0, 0
        self.fill()

    def fill(self):
        while self.begun < min(len(self.copies), self.done + self.ahead):
            self.copies[self.begun].start()
            self.begun += 1

    def take(self, count=1):
        for _ in range(count):
            self.copies[self.done].wait()
            self.done += 1
            self.fill()


class Outbox:
    def __init__(self, sems):
        self.sems, self.copies = sems, []

    def send(self, source, target):
        copy = pltpu.make_async_copy(source, target, self.sems.at[len(self.copies)])
        copy.start()
        self.copies.append(copy)

    def finish(self):
        for copy in self.copies:
            copy.wait()


def forward_layer(layer, x, length, small, weights, take, f_ref, a_ref, qkv_ref, probs_ref, mixed_ref, slope_ref):
    bq, bv, bo, g1, s1, b_in, b_out, g2, s2 = small
    wq, wk, wv, wo, w_in, w_out = weights
    rounded = x.astype(BRAIN)
    a_ref[:, :D] = rounded
    take(3)
    qkv_ref[:, 0:D] = ((dot(rounded, wq[layer]) + row(bq, layer)).astype(BRAIN) * 0.125).astype(BRAIN)
    qkv_ref[:, D : 2 * D] = dot(rounded, wk[layer]).astype(BRAIN)
    qkv_ref[:, 2 * D : 3 * D] = (dot(rounded, wv[layer]) + row(bv, layer)).astype(BRAIN)
    keys_live = live_of(length, (2 * ROWS, ROWS), 1)
    for pair in range(PAIRS):
        lanes = lambda m: slice(m * D + 128 * pair, m * D + 128 * pair + 128)
        scores = dot_right(two_heads(qkv_ref[:, lanes(0)]), qkv_ref[:, lanes(1)])
        scores = jnp.where(keys_live, scores, -1e30)
        terms = jnp.exp(scores - jnp.max(scores, axis=-1, keepdims=True))
        probs = (terms * (1.0 / jnp.sum(terms, axis=-1, keepdims=True))).astype(BRAIN)
        probs_ref[pair] = probs
        context = join_heads(dot(probs, qkv_ref[:, lanes(2)]))
        a_ref[:, A_CTX + 128 * pair : A_CTX + 128 * pair + 128] = context.astype(BRAIN)
    take(1)
    mixed = x + dot(a_ref[:, A_CTX : A_CTX + D], wo[layer]) + row(bo, layer)
    mixed_ref[...] = mixed
    hidden = centred(mixed)[0] * row(g1, layer) + row(s1, layer)
    hidden_low = hidden.astype(BRAIN)
    f_ref[:, F_HID : F_HID + D] = hidden_low
    branch = row(b_out, layer)
    for part in range(4):
        at = slice(part * D, part * D + D)
        take(2)
        pre = dot(hidden_low, w_in[layer, :, at]) + b_in[layer : layer + 1, at].astype(FLOAT)
        act, slope = gelu_pair(pre)
        act = act.astype(BRAIN)
        f_ref[:, at] = act
        slope_ref[:, at] = slope.astype(BRAIN)
        branch = branch + dot(act, w_out[layer, at, :])
    live = live_of(length, (ROWS, 1), 0)
    summed = hidden + jnp.where(live, branch.astype(BRAIN).astype(FLOAT), 0.0)
    normal, inverse = centred(summed)
    result = jnp.where(live, normal * row(g2, layer) + row(s2, layer), 0.0)
    return result, summed, normal, inverse


def feed_back(layer, grad_out, length, core, normal, inverse, g2, wi, wu, slope, g_pre, g_low, mine, f_ref, vectors, bias):
    live = live_of(length, (ROWS, 1), 0)
    grad_live = jnp.where(live, grad_out, 0.0)
    grad_summed, grad_gain, grad_shift = norm_back(grad_live, normal, inverse, row(g2, layer))
    low = jnp.where(live, grad_summed, 0.0).astype(BRAIN)
    g_low[...] = low
    vectors[layer, 5:6, :] = total(low)
    vectors[layer, 6:7, :] = grad_gain
    vectors[layer, 7:8, :] = grad_shift
    back = 0.0
    for part in range(4):
        at = slice(part * D, part * D + D)
        grads = (dot_right(low, wu[at, :]) * slope[:, at].astype(FLOAT)).astype(BRAIN)
        g_pre[:, at] = grads
        bias[layer, :, at] = total(grads)
        back = back + dot_right(grads, wi[:, at])
    for into, side, at in ((mine, core, 0), (f_ref, 1 - core, F_PRE)):
        into[:, at : at + FF // 2] = half_of(g_pre, side, FF // 2)
        into[:, at + FF // 2 : at + FF // 2 + HALF] = half_of(g_low, side, HALF)
    return grad_summed + back.astype(BRAIN).astype(FLOAT)


def attend_back(layer, grad_hidden, core, mixed, g1, qkv, probs, squares, g_all, g_context, mine, a_ref, vectors):
    wq, wk, wv, wo = squares
    normal, inverse = centred(mixed[...])
    grad_mixed, grad_gain, grad_shift = norm_back(grad_hidden, normal, inverse, row(g1, layer))
    low = grad_mixed.astype(BRAIN)
    g_all[:, 3 * D :] = low
    vectors[layer, 2:3, :] = total(low)
    vectors[layer, 3:4, :] = grad_gain
    vectors[layer, 4:5, :] = grad_shift
    g_context[...] = dot_right(low, wo[...]).astype(BRAIN)
    for pair in range(PAIRS):
        lanes = lambda m: slice(m * D + 128 * pair, m * D + 128 * pair + 128)
        context_two = two_heads(g_context[:, lanes(0)])
        probs_two = probs[pair]
        g_probs = dot_right(context_two, qkv[:, lanes(2)])
        g_all[:, lanes(2)] = dot_left(probs_two, context_two).astype(BRAIN)
        weighted = probs_two.astype(FLOAT)
        weighted_grad = weighted * g_probs
        g_raw = weighted_grad - weighted * jnp.sum(weighted_grad, axis=-1, keepdims=True)
        g_raw = g_raw.astype(BRAIN)
        g_all[:, lanes(0)] = (join_heads(dot(g_raw, qkv[:, lanes(1)])) * 0.125).astype(BRAIN)
        g_all[:, lanes(1)] = dot_left(g_raw, two_heads(qkv[:, lanes(0)])).astype(BRAIN)
    g_query, g_keys, g_values = (g_all[:, m * D : m * D + D] for m in range(3))
    vectors[layer, 0:1, :] = total(g_query)
    vectors[layer, 1:2, :] = total(g_values)
    for m in range(4):
        into = m * HALF
        mine[:, into : into + HALF] = half_of(g_all, core, HALF, m * D)
        a_ref[:, A_GRAD + into : A_GRAD + into + HALF] = half_of(g_all, 1 - core, HALF, m * D)
    return grad_mixed + dot_right(g_query, wq[...]) + dot_right(g_keys, wk[...]) + dot_right(g_values, wv[...])


def chain_kernel(lengths, x_in, bq, bv, bo, g1, s1, b_in, b_out, g2, s2, cotangent, *refs):
    big, far, refs = refs[:6], refs[6:16], refs[16:]
    vectors, bias, refs = refs[0], refs[1], refs[2:]
    near, refs = refs[:10], refs[10:]
    (qkv, probs, mixed, slope, summed, g_pre, g_low, g_all, g_context), refs = refs[:9], refs[9:]
    weights, (sems, out_sems) = refs[:6], refs[6:]
    out, flow, f0, f1, a0, a1, f_mine0, f_mine1, a_mine0, a_mine1 = near
    length, core = lengths[0], own_place()[1]
    pairs = []
    for layer in range(LAYERS):
        pairs += [(big[n].at[layer], weights[n].at[layer]) for n in range(4)]
        for k in range(4):
            at = slice(k * D, k * D + D)
            pairs.append((big[4].at[layer, :, at], weights[4].at[layer, :, at]))
            pairs.append((big[5].at[layer, at, :], weights[5].at[layer, at, :]))
    stream, outbox = Stream(pairs, sems, 8), Outbox(out_sems)
    small = (bq, bv, bo, g1, s1, b_in, b_out, g2, s2)
    give = lambda *which: [outbox.send(near[n], far[n]) for n in which]
    x = x_in[...]
    for layer, (f_ref, a_ref) in enumerate(((f0, a0), (f1, a1))):
        x, total_sum, normal, inverse = forward_layer(layer, x, length, small, weights, stream.take, f_ref, a_ref,
                                                      qkv.at[layer], probs.at[layer], mixed.at[layer], slope.at[layer])
        if layer == 0:
            summed[...] = total_sum
    out[...] = x
    give(0)
    grad = cotangent[...]
    for layer, f_ref, a_ref, f_mine, a_mine in ((1, f1, a1, f_mine1, a_mine1), (0, f0, a0, f_mine0, a_mine0)):
        if layer == 0:
            normal, inverse = centred(summed[...])
        grad = feed_back(layer, grad, length, core, normal, inverse, g2, weights[4].at[layer], weights[5].at[layer], slope.at[layer],
                         g_pre, g_low, f_mine, f_ref, vectors, bias)
        give(2 + layer, 6 + layer)
        grad = attend_back(layer, grad, core, mixed.at[layer], g1, qkv.at[layer], probs.at[layer], [w.at[layer] for w in weights[:4]],
                           g_all, g_context, a_mine, a_ref, vectors)
        give(4 + layer, 8 + layer)
    flow[...] = grad
    give(1)
    outbox.finish()


def loads(pairs):
    return [(source, target.at[ROWS * n : ROWS * n + ROWS]) for sources, target in pairs for n, source in enumerate(sources)]


def lane_blocks(values):
    return [values[:, 128 * j : 128 * j + 128] for j in range(values.shape[1] // 128)]


def give(outbox, buffer, send, keep):
    outbox.send(buffer.at[CHIPS // 2 :], send)
    outbox.send(buffer.at[: CHIPS // 2], keep)


def feed_grad_kernel(own, got, mine, send_c, keep_c, send_b, keep_b,
                     act, low, hidden, pre, buffer_c, buffer_b, sems, out_sems):
    x_of = lambda at, width: (own.at[:, at : at + width], got.at[:, at : at + width])
    f_of = lambda at, width: (mine.at[:, at : at + width], got.at[:, F_PRE + at : F_PRE + at + width])
    pieces = [slice(k * D, k * D + D) for k in range(4)]
    pairs = [(f_of(FF // 2, HALF), low)] + [(x_of(k * D, D), act.at[:, pieces[k]]) for k in range(4)]
    pairs += [(f_of(0, FF // 2), pre), (x_of(F_HID, D), hidden)]
    stream, outbox = Stream(loads(pairs), sems, 14), Outbox(out_sems)
    slot_c, slot_b = slots_of(0), slots_of(1)
    stream.take(2)
    for k in range(4):
        stream.take(2)
        grads = dot_left(act[:, pieces[k]], low[...]).astype(BRAIN)
        for n in range(16):
            slot = slot_c(k * 16 + n)
            for j in range(3):
                buffer_c[slot, 48 * j : 48 * j + 48] = grads[48 * n : 48 * n + 48, 128 * j : 128 * j + 128]
    give(outbox, buffer_c, send_c, keep_c)
    stream.take(4)
    for k in range(2):
        blocks = lane_blocks(dot_left(hidden[:, k * HALF : k * HALF + HALF], pre[...]))
        for n in range(32):
            chunk = jnp.concatenate([b[12 * n : 12 * n + 12] for b in blocks], axis=0)
            buffer_b[slot_b(k * 32 + n)] = chunk.astype(BRAIN)
    give(outbox, buffer_b, send_b, keep_b)
    outbox.finish()


def attend_grad_kernel(layer, vectors, bias, own, got, mine, send, keep,
                       x_in, context, grads, buffer, turned, sems, out_sems):
    x_of = lambda at, width: (own.at[:, at : at + width], got.at[:, at : at + width])
    stream = Stream(loads([((mine, got.at[:, A_GRAD:]), grads), (x_of(0, D), x_in), (x_of(A_CTX, D), context)]), sems, 6)
    outbox = Outbox(out_sems)
    slot_a = slots_of(2)
    turned[...] = jnp.concatenate([vectors[layer], jnp.zeros((120, D), FLOAT)], axis=0).T
    for n in range(DEVICES):
        turned[6 * n : 6 * n + 1, 64:88] = bias[layer, :, 24 * n : 24 * n + 24]
    stream.take(6)
    for k in range(2):
        at = slice(k * HALF, k * HALF + HALF)
        blocks = lane_blocks(dot_left(x_in[:, at], grads[:, : 3 * HALF])) + lane_blocks(dot_left(context[:, at], grads[:, 3 * HALF :]))
        blocks.append(turned[at, :])
        for n in range(32):
            chunk = jnp.concatenate([b[12 * n : 12 * n + 12] for b in blocks] + [jnp.zeros((4, 128), FLOAT)], axis=0)
            buffer[slot_a(k * 32 + n)] = chunk.astype(BRAIN)
    give(outbox, buffer, send, keep)
    outbox.finish()


A_ROWS, B_ROWS, C_ROWS = 160, 144, 144
ALL_ROWS = A_ROWS + B_ROWS + C_ROWS
OWN_ROWS = 25 * 6 + 3 * 24


def merge_kernel(a_keep, a_got, b_keep, b_got, c_keep, c_got, keep, send):
    at = 0
    for rows, mine, got in ((A_ROWS, a_keep, a_got), (B_ROWS, b_keep, b_got), (C_ROWS, c_keep, c_got)):
        summed = (mine[...].astype(FLOAT) + got[...].astype(FLOAT)).astype(BRAIN)
        keep[:, at : at + rows] = summed[:4]
        send[:, at : at + rows] = summed[4:]
        at += rows


def merge(a, b, c):
    out = shape(4, ALL_ROWS, 128)
    return small_call(merge_kernel, [out, out], (*a, *b, *c))


def last_kernel(keep0, got0, keep1, got1, mine, theirs):
    core = own_place()[1]
    for layer, (keep, got) in enumerate(((keep0, got0), (keep1, got1))):
        summed = keep[0].astype(FLOAT) + got[0].astype(FLOAT)
        low, high = [], []
        starts = [12 * p for p in range(13)] + [A_ROWS + 12 * p for p in range(12)]
        for start in starts:
            low.append(summed[start : start + 6])
            high.append(summed[start + 6 : start + 12])
        for j in range(3):
            start = A_ROWS + B_ROWS + 48 * j
            low.append(summed[start : start + 24])
            high.append(summed[start + 24 : start + 48])
        fill = jnp.zeros((2, 128), FLOAT)
        low, high = jnp.concatenate(low + [fill], axis=0), jnp.concatenate(high + [fill], axis=0)
        mine[layer] = jnp.where(core == 0, low, high)
        theirs[layer] = jnp.where(core == 0, high, low).astype(BRAIN)


def place_kernel(mine, got, wq, bq, wk, wv, bv, wo, bo, g1, s1, w_in, b_in, w_out, b_out, g2, s2):
    core = own_place()[1]
    for layer in range(LAYERS):
        own, other = mine[layer], got[layer].astype(FLOAT)
        sides = (jnp.where(core == 0, own, other), jnp.where(core == 0, other, own))
        for side, rows in enumerate(sides):
            for m, ref in enumerate((wq, wk, wv, wo)):
                for j in range(3):
                    at = 6 * (3 * m + j)
                    ref[:, layer, 384 * side + 128 * j : 384 * side + 128 * j + 128] = rows[at : at + 6]
            for j in range(12):
                at, lane = 6 * (13 + j), 1536 * side + 128 * j
                w_in[:, layer, lane : lane + 128] = rows[at : at + 6]
            for j in range(3):
                at, lane = 150 + 24 * j, 384 * side + 128 * j
                w_out[layer, :, lane : lane + 128] = rows[at : at + 24]
        vectors = own[72:78] + other[72:78]
        turned = jnp.concatenate([vectors, jnp.zeros((122, 128), FLOAT)], axis=0).T
        for n, ref in enumerate((bq, bv, bo, g1, s1, b_out, g2, s2)):
            ref[layer : layer + 1, :] = turned[n : n + 1, 0:6]
        b_in[layer : layer + 1, :] = vectors[0:1, 64:88]


def shape(*dims, kind=BRAIN):
    return jax.ShapeDtypeStruct(dims, kind)


VMEM = pl.BlockSpec(memory_space=pltpu.VMEM)
SMEM = pl.BlockSpec(memory_space=pltpu.SMEM)
HBM = pl.BlockSpec(memory_space=pltpu.HBM)


DW_LIMIT = 24


def call(kernel, ins, outs, scratch, args, micros, limit=63):
    outs = [o if isinstance(o, tuple) else (o, VMEM) for o in outs]
    return pl.pallas_call(
        kernel,
        in_specs=ins,
        out_specs=[o[1] for o in outs],
        out_shape=[o[0] for o in outs],
        scratch_shapes=scratch,
        compiler_params=pltpu.CompilerParams(vmem_limit_bytes=limit * 2**20),
        cost_estimate=pl.CostEstimate(flops=micros * 10**9, bytes_accessed=2**20, transcendentals=0),
    )(*args)


def small_call(kernel, outs, args):
    return call(kernel, [VMEM] * len(args), outs, [], args, 1, 12)


def held(kind, *dims):
    return pltpu.VMEM(dims, kind)


def feed_grads(own, got, mine, *after):
    out = shape(CHIPS // 2, C_ROWS, 128)
    buffer = held(BRAIN, CHIPS, C_ROWS, 128)
    both = 2 * ROWS
    parts = call(
        lambda *refs: feed_grad_kernel(*refs[:3], *refs[3 + len(after) :]),
        [HBM] * (3 + len(after)),
        [(out, HBM)] * 4,
        [held(BRAIN, both, FF), held(BRAIN, both, HALF), held(BRAIN, both, D), held(BRAIN, both, FF // 2), buffer, buffer,
         pltpu.SemaphoreType.DMA((14,)), pltpu.SemaphoreType.DMA((4,))],
        (own, got, mine, *after),
        6,
        DW_LIMIT,
    )
    return parts[:2], parts[2:]


def attend_grads(layer, own, got, mine, vectors, bias, *after):
    out = shape(CHIPS // 2, A_ROWS, 128)
    both = 2 * ROWS
    return call(
        lambda *refs: attend_grad_kernel(layer, *refs[:5], *refs[5 + len(after) :]),
        [VMEM] * 2 + [HBM] * (3 + len(after)),
        [(out, HBM)] * 2,
        [held(BRAIN, both, D), held(BRAIN, both, D), held(BRAIN, both, 4 * HALF), held(BRAIN, CHIPS, A_ROWS, 128), held(FLOAT, D, 128),
         pltpu.SemaphoreType.DMA((6,)), pltpu.SemaphoreType.DMA((2,))],
        (vectors, bias, own, got, mine, *after),
        5,
        DW_LIMIT,
    )


def body(inputs, lengths, wq, bq, wk, wv, bv, wo, bo, g1, s1, w_in, b_in, w_out, b_out, g2, s2, cotangent):
    wide, f_shape, a_shape = shape(ROWS, D, kind=FLOAT), shape(ROWS, F_WIDTH), shape(ROWS, A_WIDTH)
    f_mine, a_mine = shape(ROWS, FF // 2 + HALF), shape(ROWS, 4 * HALF)
    far = [wide, wide, f_shape, f_shape, a_shape, a_shape, f_mine, f_mine, a_mine, a_mine]
    out, flow, f0, f1, a0, a1, f_mine0, f_mine1, a_mine0, a_mine1, vectors, bias = call(
        chain_kernel,
        [SMEM] + [VMEM] * 11 + [HBM] * 6,
        [(s, HBM) for s in far] + [shape(LAYERS, 8, D, kind=FLOAT), shape(LAYERS, 1, FF, kind=FLOAT)],
        [pltpu.VMEM(s.shape, s.dtype) for s in far]
        + [held(BRAIN, LAYERS, ROWS, 3 * D), held(BRAIN, LAYERS, PAIRS, 2 * ROWS, ROWS), held(FLOAT, LAYERS, ROWS, D), held(BRAIN, LAYERS, ROWS, FF)]
        + [held(FLOAT, ROWS, D), held(BRAIN, ROWS, FF), held(BRAIN, ROWS, D), held(BRAIN, ROWS, 4 * D), held(BRAIN, ROWS, D)]
        + [held(BRAIN, LAYERS, D, D)] * 4
        + [held(BRAIN, LAYERS, D, FF), held(BRAIN, LAYERS, FF, D)]
        + [pltpu.SemaphoreType.DMA((24,)), pltpu.SemaphoreType.DMA((10,))],
        (lengths, inputs.reshape(ROWS, D), bq, bv, bo, g1, s1, b_in, b_out, g2, s2, cotangent.reshape(ROWS, D), wq, wk, wv, wo, w_in, w_out),
        30,
    )
    c1, b1 = feed_grads(f1, core_swap(f1), f_mine1)
    a1 = attend_grads(1, a1, core_swap(a1), a_mine1, vectors, bias, c1[0])
    c0, b0 = feed_grads(f0, core_swap(f0), f_mine0, a1[0])
    a0 = attend_grads(0, a0, core_swap(a0), a_mine0, vectors, bias, c0[0])
    ends = []
    for a, b, c in ((a0, b0, c0), (a1, b1, c1)):
        ends += cube_end([cube_start(*a, 2), cube_start(*b, 1), cube_start(*c, 0)])
    own = shape(LAYERS, OWN_ROWS + 2, 128, kind=FLOAT)
    mine, theirs = small_call(last_kernel, [own, shape(LAYERS, OWN_ROWS + 2, 128)], ends)
    matrix, vector = shape(6, LAYERS, D, kind=FLOAT), shape(LAYERS, 6, kind=FLOAT)
    grads = small_call(
        place_kernel,
        [matrix, vector, matrix, matrix, vector, matrix, vector, vector, vector, shape(6, LAYERS, FF, kind=FLOAT),
                   shape(LAYERS, 24, kind=FLOAT), shape(LAYERS, 24, D, kind=FLOAT), vector, vector, vector],
        (mine, core_swap(theirs)),
    )
    turned = (0, 2, 3, 5, 9)
    grads = [g.swapaxes(0, 1) if n in turned else g for n, g in enumerate(grads)]
    return (out.reshape(inputs.shape), flow.reshape(inputs.shape), *grads)


def solution(mesh):
    rows = P(AXES, None, None)
    in_specs = (rows, P(AXES)) + (P(),) * 15 + (rows,)
    wide, thin = P(None, AXES, None), P(None, AXES)
    out_specs = (rows, rows, wide, thin, wide, wide, thin, wide, thin, thin, thin, wide, thin, wide, thin, thin, thin)
    return jax.shard_map(body, mesh=mesh, in_specs=in_specs, out_specs=out_specs, check_vma=False)
```

```python
import jax
import jax.numpy as jnp
import numpy as np
from jax import lax
from jax.experimental import pallas as pl
from jax.experimental.pallas import tpu as pltpu
from jax.sharding import PartitionSpec as P

PAIRS = 6
LAYERS = 2
ROWS = 160
D = 768
FF = 3072
HALF = 384
EPSILON = 1e-12
FLOAT = jnp.float32
BRAIN = jnp.bfloat16
AXES = ("dp", "seq")
DEVICES = 128
CHIPS = 64


def flip(index, dim):
    core, y, x, z = index & 1, (index >> 1) & 3, (index >> 3) & 3, (index >> 5) & 3
    other = lambda i: i ^ 1 if dim < 3 else 3 - i
    if dim % 3 == 0:
        x = other(x)
    elif dim % 3 == 1:
        y = other(y)
    else:
        z = other(z)
    return z * 32 + x * 8 + y * 2 + core


def bit_of(chip, dim):
    coordinate = ((chip >> 2) & 3, chip & 3, chip >> 4)[dim % 3]
    return ((coordinate ^ (coordinate >> 1)) >> (dim // 3)) & 1


SHIFT = (0, 0)


def dim_at(part, step, core):
    layer, part = divmod(part, 3)
    return (part + step + SHIFT[layer]) % 3 + 3 * core if step < 3 else (step + layer) % 3 + 3 * (1 - core)


def slot_base(part, core, chip):
    return sum(bit_of(chip, dim_at(part, step, core)) << (5 - step) for step in range(6))


def own_place():
    index = lax.axis_index(AXES[0]) * 8 + lax.axis_index(AXES[1])
    return index // 2, index % 2


def slots_of(part):
    chip, core = own_place()
    own = jnp.where(core == 0, slot_base(part, 0, chip), slot_base(part, 1, chip))
    return lambda other: jnp.where(core == 0, slot_base(part, 0, other), slot_base(part, 1, other)) ^ own


def cube_send(values, part, *steps):
    pairs = []
    for start in range(DEVICES):
        end = start
        for step in steps:
            end = flip(end, dim_at(part, step, start & 1))
        pairs.append((start, end))
    return lax.ppermute(values, AXES, pairs)


def core_swap(values):
    return lax.ppermute(values, AXES, [(i, i ^ 1) for i in range(DEVICES)])


def add_low(left, right):
    return (left.astype(FLOAT) + right.astype(FLOAT)).astype(BRAIN)


def split_sum(keep, got):
    half = keep.shape[0] // 2
    return add_low(keep[:half], got[:half]), add_low(keep[half:], got[half:])


class Turns:
    def __init__(self, last):
        self.last = last

    def sum(self, keep, got):
        got, _ = lax.optimization_barrier((got, self.last))
        keep, send = split_sum(keep, got)
        self.last = send
        return keep, send

    def merge(self, parts):
        keeps, gots = [p[0] for p in parts], [p[1] for p in parts]
        gots, _ = lax.optimization_barrier((gots, self.last))
        quarters = merge(*[pair for pair in zip(keeps, gots)])
        self.last = quarters[3]
        return quarters

    def sum_four(self, keep, gots):
        gots, _ = lax.optimization_barrier((gots, self.last))
        whole = sum([got.astype(FLOAT) for got in gots], keep.astype(FLOAT)).astype(BRAIN)
        keep, send = whole[:1], whole[1:]
        self.last = send
        return keep, send


def cube_sums(parts, last):
    turns = Turns(last)
    sent = {}
    for layer in (1, 0):
        sent[layer] = [[keep, cube_send(send, 3 * layer + n, 0)] for n, (send, keep) in enumerate(parts[layer])]
    for step in (1, 2):
        for layer in (1, 0):
            for n, (keep, got) in enumerate(sent[layer]):
                keep, send = turns.sum(keep, got)
                sent[layer][n] = [keep, cube_send(send, 3 * layer + n, step)]
    for layer in (1, 0):
        c, b, a = sent[layer]
        quarters = turns.merge((a, b, c))
        across = ((4,), (3,), (3, 4))
        sent[layer] = [quarters[0], [cube_send(q, 3 * layer, *steps) for q, steps in zip(quarters[1:], across)]]
    for layer in (1, 0):
        keep, send = turns.sum_four(*sent[layer])
        sent[layer] = [keep, cube_send(send, 3 * layer, 5)]
    return sent


def dot(left, right):
    return lax.dot_general(left, right, (((1,), (0,)), ((), ())), preferred_element_type=FLOAT)


def dot_right(left, right):
    return lax.dot_general(left, right, (((1,), (1,)), ((), ())), preferred_element_type=FLOAT)


def dot_left(left, right):
    return lax.dot_general(left, right, (((0,), (0,)), ((), ())), preferred_element_type=FLOAT)


def centred(values):
    centre = values - jnp.mean(values, axis=-1, keepdims=True)
    inverse = lax.rsqrt(jnp.mean(centre * centre, axis=-1, keepdims=True) + EPSILON)
    return centre * inverse, inverse


def norm_back(grad, normal, inverse, gain):
    scaled = grad * gain
    back = scaled - jnp.mean(scaled, axis=-1, keepdims=True)
    back = back - normal * jnp.mean(scaled * normal, axis=-1, keepdims=True)
    return back * inverse, total(grad * normal), total(grad)


def total(values):
    return jnp.sum(values.astype(FLOAT), axis=0, keepdims=True)


def row(ref, layer):
    return ref[layer : layer + 1, :].astype(FLOAT)


def gelu_pair(values):
    cdf = 0.5 + 0.5 * lax.erf(values * np.float32(0.5**0.5))
    density = jnp.exp(-0.5 * values * values) * np.float32((2 * np.pi) ** -0.5)
    return values * cdf, cdf + values * density


def live_of(length, shape, axis):
    return lax.broadcasted_iota(jnp.int32, shape, axis) < length


def two_heads(pair):
    first = lax.broadcasted_iota(jnp.int32, pair.shape, 1) < 64
    none = jnp.zeros_like(pair)
    return jnp.concatenate([jnp.where(first, pair, none), jnp.where(first, none, pair)], axis=0)


def join_heads(both):
    first = lax.broadcasted_iota(jnp.int32, (ROWS, 128), 1) < 64
    return jnp.where(first, both[:ROWS], both[ROWS:])


def half_of(ref, core, width, at=0):
    return ref[:, pl.ds(pl.multiple_of(at + core * width, 128), width)]


F_HID, F_PRE, F_LOW = FF, FF + D, FF + D + FF // 2
F_WIDTH = FF + D + FF // 2 + HALF
A_CTX, A_GRAD = D, 2 * D
A_WIDTH = 2 * D + 4 * HALF
A1_AT, F0_AT, A0_AT = 0, A_WIDTH, A_WIDTH + F_WIDTH
REST = 2 * A_WIDTH + F_WIDTH


class Stream:
    def __init__(self, pairs, sems, ahead):
        self.copies = [pltpu.make_async_copy(source, target, sems.at[n]) for n, (source, target) in enumerate(pairs)]
        self.ahead, self.done, self.begun = ahead, 0, 0
        self.fill()

    def fill(self):
        while self.begun < min(len(self.copies), self.done + self.ahead):
            self.copies[self.begun].start()
            self.begun += 1

    def take(self, count=1):
        for _ in range(count):
            self.copies[self.done].wait()
            self.done += 1
            self.fill()


class Outbox:
    def __init__(self, sems):
        self.sems, self.copies = sems, []

    def send(self, source, target):
        copy = pltpu.make_async_copy(source, target, self.sems.at[len(self.copies)])
        copy.start()
        self.copies.append(copy)

    def finish(self):
        for copy in self.copies:
            copy.wait()


def forward_layer(layer, x, length, small, weights, take, f_ref, a_ref, qkv_ref, probs_ref, mixed_ref, slope_ref):
    bq, bv, bo, g1, s1, b_in, b_out, g2, s2 = small
    wq, wk, wv, wo, w_in, w_out = weights
    rounded = x.astype(BRAIN)
    a_ref[:, :D] = rounded
    take(3)
    qkv_ref[:, 0:D] = ((dot(rounded, wq[layer]) + row(bq, layer)).astype(BRAIN) * 0.125).astype(BRAIN)
    qkv_ref[:, D : 2 * D] = dot(rounded, wk[layer]).astype(BRAIN)
    qkv_ref[:, 2 * D : 3 * D] = (dot(rounded, wv[layer]) + row(bv, layer)).astype(BRAIN)
    keys_live = live_of(length, (2 * ROWS, ROWS), 1)
    lanes = lambda m, pair: slice(m * D + 128 * pair, m * D + 128 * pair + 128)
    scores = [dot_right(two_heads(qkv_ref[:, lanes(0, n)]), qkv_ref[:, lanes(1, n)]) for n in range(PAIRS)]
    for pair in range(PAIRS):
        masked = jnp.where(keys_live, scores[pair], -1e30)
        terms = jnp.exp(masked - jnp.max(masked, axis=-1, keepdims=True))
        probs_ref[pair] = (terms * (1.0 / jnp.sum(terms, axis=-1, keepdims=True))).astype(BRAIN)
    for pair in range(PAIRS):
        context = join_heads(dot(probs_ref[pair], qkv_ref[:, lanes(2, pair)]))
        a_ref[:, A_CTX + 128 * pair : A_CTX + 128 * pair + 128] = context.astype(BRAIN)
    take(1)
    mixed = x + dot(a_ref[:, A_CTX : A_CTX + D], wo[layer]) + row(bo, layer)
    mixed_ref[...] = mixed
    hidden = centred(mixed)[0] * row(g1, layer) + row(s1, layer)
    hidden_low = hidden.astype(BRAIN)
    f_ref[:, F_HID : F_HID + D] = hidden_low
    branch = row(b_out, layer)
    for part in range(4):
        at = slice(part * D, part * D + D)
        take(2)
        pre = dot(hidden_low, w_in[layer, :, at]) + b_in[layer : layer + 1, at].astype(FLOAT)
        act, slope = gelu_pair(pre)
        act = act.astype(BRAIN)
        f_ref[:, at] = act
        slope_ref[:, at] = slope.astype(BRAIN)
        branch = branch + dot(act, w_out[layer, at, :])
    live = live_of(length, (ROWS, 1), 0)
    summed = hidden + jnp.where(live, branch.astype(BRAIN).astype(FLOAT), 0.0)
    normal, inverse = centred(summed)
    result = jnp.where(live, normal * row(g2, layer) + row(s2, layer), 0.0)
    return result, summed, normal, inverse


def feed_back(layer, grad_out, length, core, normal, inverse, g2, wi, wu, slope, g_pre, g_low, mine, f_ref, vectors, bias):
    live = live_of(length, (ROWS, 1), 0)
    grad_live = jnp.where(live, grad_out, 0.0)
    grad_summed, grad_gain, grad_shift = norm_back(grad_live, normal, inverse, row(g2, layer))
    low = jnp.where(live, grad_summed, 0.0).astype(BRAIN)
    g_low[...] = low
    vectors[layer, 5:6, :] = total(low)
    vectors[layer, 6:7, :] = grad_gain
    vectors[layer, 7:8, :] = grad_shift
    back = 0.0
    for part in range(4):
        at = slice(part * D, part * D + D)
        grads = (dot_right(low, wu[at, :]) * slope[:, at].astype(FLOAT)).astype(BRAIN)
        g_pre[:, at] = grads
        bias[layer, :, at] = total(grads)
        back = back + dot_right(grads, wi[:, at])
    for into, side, at in ((mine, core, 0), (f_ref, 1 - core, F_PRE)):
        into[:, at : at + FF // 2] = half_of(g_pre, side, FF // 2)
        into[:, at + FF // 2 : at + FF // 2 + HALF] = half_of(g_low, side, HALF)
    return grad_summed + back.astype(BRAIN).astype(FLOAT)


def attend_back(layer, grad_hidden, core, mixed, g1, qkv, probs, squares, g_all, g_context, mine, a_ref, vectors, ready):
    wq, wk, wv, wo = squares
    normal, inverse = centred(mixed[...])
    grad_mixed, grad_gain, grad_shift = norm_back(grad_hidden, normal, inverse, row(g1, layer))
    low = grad_mixed.astype(BRAIN)
    g_all[:, 3 * D :] = low
    vectors[layer, 2:3, :] = total(low)
    vectors[layer, 3:4, :] = grad_gain
    vectors[layer, 4:5, :] = grad_shift
    g_context[...] = dot_right(low, wo[...]).astype(BRAIN)
    lanes = lambda m, pair: slice(m * D + 128 * pair, m * D + 128 * pair + 128)
    context_two = [two_heads(g_context[:, lanes(0, n)]) for n in range(PAIRS)]
    g_probs = [dot_right(context_two[n], qkv[:, lanes(2, n)]) for n in range(PAIRS)]
    for pair in range(PAIRS):
        g_all[:, lanes(2, pair)] = dot_left(probs[pair], context_two[pair]).astype(BRAIN)
    g_raws = []
    for pair in range(PAIRS):
        weighted = probs[pair].astype(FLOAT)
        weighted_grad = weighted * g_probs[pair]
        g_raws.append((weighted_grad - weighted * jnp.sum(weighted_grad, axis=-1, keepdims=True)).astype(BRAIN))
    for pair in range(PAIRS):
        g_all[:, lanes(0, pair)] = (join_heads(dot(g_raws[pair], qkv[:, lanes(1, pair)])) * 0.125).astype(BRAIN)
    for pair in range(PAIRS):
        g_all[:, lanes(1, pair)] = dot_left(g_raws[pair], two_heads(qkv[:, lanes(0, pair)])).astype(BRAIN)
    g_query, g_keys, g_values = (g_all[:, m * D : m * D + D] for m in range(3))
    vectors[layer, 0:1, :] = total(g_query)
    vectors[layer, 1:2, :] = total(g_values)
    for m in range(4):
        into = m * HALF
        mine[:, into : into + HALF] = half_of(g_all, core, HALF, m * D)
        a_ref[:, A_GRAD + into : A_GRAD + into + HALF] = half_of(g_all, 1 - core, HALF, m * D)
    ready()
    return grad_mixed + dot_right(g_query, wq[...]) + dot_right(g_keys, wk[...]) + dot_right(g_values, wv[...])


AHEAD = 6


def chain_kernel(lengths, x_in, bq, bv, bo, g1, s1, b_in, b_out, g2, s2, cotangent, *refs):
    big, far, refs = refs[:6], refs[6:14], refs[14:]
    vectors, bias, refs = refs[0], refs[1], refs[2:]
    near, refs = refs[:8], refs[8:]
    (qkv, probs, mixed, slope, summed, g_pre, g_low, g_all, g_context), refs = refs[:9], refs[9:]
    weights, (sems, out_sems) = refs[:6], refs[6:]
    out, flow, f1, rest, f_mine0, f_mine1, a_mine0, a_mine1 = near
    a1, f0, a0 = (rest.at[:, at : at + width] for at, width in ((A1_AT, A_WIDTH), (F0_AT, F_WIDTH), (A0_AT, A_WIDTH)))
    length, core = lengths[0], own_place()[1]
    pairs = []
    for layer in range(LAYERS):
        pairs += [(big[n].at[layer], weights[n].at[layer]) for n in range(4)]
        for k in range(4):
            at = slice(k * D, k * D + D)
            pairs.append((big[4].at[layer, :, at], weights[4].at[layer, :, at]))
            pairs.append((big[5].at[layer, at, :], weights[5].at[layer, at, :]))
    stream, outbox = Stream(pairs, sems, AHEAD), Outbox(out_sems)
    small = (bq, bv, bo, g1, s1, b_in, b_out, g2, s2)
    give = lambda *which: [outbox.send(near[n], far[n]) for n in which]
    give_rest = lambda at, width: outbox.send(rest.at[:, at : at + width], far[3].at[:, at : at + width])
    give_a = lambda layer: (give(6 + layer), give_rest(A1_AT if layer == 1 else A0_AT, A_WIDTH))
    give_f = lambda layer: give(2) if layer == 1 else give_rest(F0_AT, F_WIDTH)
    x = x_in[...]
    for layer, (f_ref, a_ref) in enumerate(((f0, a0), (f1, a1))):
        x, total_sum, normal, inverse = forward_layer(layer, x, length, small, weights, stream.take, f_ref, a_ref,
                                                      qkv.at[layer], probs.at[layer], mixed.at[layer], slope.at[layer])
        if layer == 0:
            summed[...] = total_sum
    out[...] = x
    give(0)
    grad = cotangent[...]
    for layer, f_ref, a_ref, f_mine, a_mine in ((1, f1, a1, f_mine1, a_mine1), (0, f0, a0, f_mine0, a_mine0)):
        if layer == 0:
            normal, inverse = centred(summed[...])
        grad = feed_back(layer, grad, length, core, normal, inverse, g2, weights[4].at[layer], weights[5].at[layer], slope.at[layer],
                         g_pre, g_low, f_mine, f_ref, vectors, bias)
        give(4 + layer)
        give_f(layer)
        grad = attend_back(layer, grad, core, mixed.at[layer], g1, qkv.at[layer], probs.at[layer], [w.at[layer] for w in weights[:4]],
                           g_all, g_context, a_mine, a_ref, vectors, lambda layer=layer: give_a(layer))
    flow[...] = grad
    give(1)
    outbox.finish()


def loads(pairs):
    return [(source, target.at[ROWS * n : ROWS * n + ROWS]) for sources, target in pairs for n, source in enumerate(sources)]


def lane_blocks(values):
    return [values[:, 128 * j : 128 * j + 128] for j in range(values.shape[1] // 128)]


def give(outbox, buffer, send, keep):
    outbox.send(buffer.at[CHIPS // 2 :], send)
    outbox.send(buffer.at[: CHIPS // 2], keep)


def feed_grad_kernel(layer, base, own, got, mine, send_c, keep_c, send_b, keep_b,
                     act, low, hidden, pre, buffer_c, buffer_b, sems, out_sems):
    x_of = lambda at, width: tuple(ref.at[:, base + at : base + at + width] for ref in (own, got))
    f_of = lambda at, width: (mine.at[:, at : at + width], got.at[:, base + F_PRE + at : base + F_PRE + at + width])
    pieces = [slice(k * D, k * D + D) for k in range(4)]
    pairs = [(f_of(FF // 2, HALF), low)] + [(x_of(k * D, D), act.at[:, pieces[k]]) for k in range(4)]
    pairs += [(f_of(0, FF // 2), pre), (x_of(F_HID, D), hidden)]
    stream, outbox = Stream(loads(pairs), sems, 14), Outbox(out_sems)
    slot_c, slot_b = slots_of(3 * layer), slots_of(3 * layer + 1)
    stream.take(2)
    for k in range(4):
        stream.take(2)
        grads = dot_left(act[:, pieces[k]], low[...]).astype(BRAIN)
        for n in range(16):
            slot = slot_c(k * 16 + n)
            for j in range(3):
                buffer_c[slot, 48 * j : 48 * j + 48] = grads[48 * n : 48 * n + 48, 128 * j : 128 * j + 128]
    give(outbox, buffer_c, send_c, keep_c)
    stream.take(4)
    for k in range(2):
        blocks = lane_blocks(dot_left(hidden[:, k * HALF : k * HALF + HALF], pre[...]))
        for n in range(32):
            chunk = jnp.concatenate([b[12 * n : 12 * n + 12] for b in blocks], axis=0)
            buffer_b[slot_b(k * 32 + n)] = chunk.astype(BRAIN)
    give(outbox, buffer_b, send_b, keep_b)
    outbox.finish()


def attend_grad_kernel(layer, base, vectors, bias, own, got, mine, send, keep,
                       x_in, context, grads, buffer, turned, sems, out_sems):
    x_of = lambda at, width: tuple(ref.at[:, base + at : base + at + width] for ref in (own, got))
    stream = Stream(loads([((mine, got.at[:, base + A_GRAD : base + A_WIDTH]), grads), (x_of(0, D), x_in), (x_of(A_CTX, D), context)]), sems, 6)
    outbox = Outbox(out_sems)
    slot_a = slots_of(3 * layer + 2)
    turned[...] = jnp.concatenate([vectors[layer], jnp.zeros((120, D), FLOAT)], axis=0).T
    for n in range(DEVICES):
        turned[6 * n : 6 * n + 1, 64:88] = bias[layer, :, 24 * n : 24 * n + 24]
    stream.take(6)
    for k in range(2):
        at = slice(k * HALF, k * HALF + HALF)
        blocks = lane_blocks(dot_left(x_in[:, at], grads[:, : 3 * HALF])) + lane_blocks(dot_left(context[:, at], grads[:, 3 * HALF :]))
        blocks.append(turned[at, :])
        for n in range(32):
            chunk = jnp.concatenate([b[12 * n : 12 * n + 12] for b in blocks] + [jnp.zeros((4, 128), FLOAT)], axis=0)
            buffer[slot_a(k * 32 + n)] = chunk.astype(BRAIN)
    give(outbox, buffer, send, keep)
    outbox.finish()


A_ROWS, B_ROWS, C_ROWS = 160, 144, 144
ALL_ROWS = A_ROWS + B_ROWS + C_ROWS
OWN_ROWS = 25 * 6 + 3 * 24


def merge_kernel(a_keep, a_got, b_keep, b_got, c_keep, c_got, *quarters):
    at = 0
    for rows, mine, got in ((A_ROWS, a_keep, a_got), (B_ROWS, b_keep, b_got), (C_ROWS, c_keep, c_got)):
        summed = (mine[...].astype(FLOAT) + got[...].astype(FLOAT)).astype(BRAIN)
        for n, quarter in enumerate(quarters):
            quarter[:, at : at + rows] = summed[2 * n : 2 * n + 2]
        at += rows


def merge(a, b, c):
    return small_call(merge_kernel, [shape(2, ALL_ROWS, 128)] * 4, (*a, *b, *c))


def last_kernel(keep0, got0, keep1, got1, mine, theirs):
    core = own_place()[1]
    for layer, (keep, got) in enumerate(((keep0, got0), (keep1, got1))):
        summed = keep[0].astype(FLOAT) + got[0].astype(FLOAT)
        low, high = [], []
        starts = [12 * p for p in range(13)] + [A_ROWS + 12 * p for p in range(12)]
        for start in starts:
            low.append(summed[start : start + 6])
            high.append(summed[start + 6 : start + 12])
        for j in range(3):
            start = A_ROWS + B_ROWS + 48 * j
            low.append(summed[start : start + 24])
            high.append(summed[start + 24 : start + 48])
        fill = jnp.zeros((2, 128), FLOAT)
        low, high = jnp.concatenate(low + [fill], axis=0), jnp.concatenate(high + [fill], axis=0)
        mine[layer] = jnp.where(core == 0, low, high)
        theirs[layer] = jnp.where(core == 0, high, low).astype(BRAIN)


def place_kernel(mine, got, wq, bq, wk, wv, bv, wo, bo, g1, s1, w_in, b_in, w_out, b_out, g2, s2):
    core = own_place()[1]
    for layer in range(LAYERS):
        own, other = mine[layer], got[layer].astype(FLOAT)
        sides = (jnp.where(core == 0, own, other), jnp.where(core == 0, other, own))
        for side, rows in enumerate(sides):
            for m, ref in enumerate((wq, wk, wv, wo)):
                for j in range(3):
                    at = 6 * (3 * m + j)
                    ref[:, layer, 384 * side + 128 * j : 384 * side + 128 * j + 128] = rows[at : at + 6]
            for j in range(12):
                at, lane = 6 * (13 + j), 1536 * side + 128 * j
                w_in[:, layer, lane : lane + 128] = rows[at : at + 6]
            for j in range(3):
                at, lane = 150 + 24 * j, 384 * side + 128 * j
                w_out[layer, :, lane : lane + 128] = rows[at : at + 24]
        vectors = own[72:78] + other[72:78]
        turned = jnp.concatenate([vectors, jnp.zeros((122, 128), FLOAT)], axis=0).T
        for n, ref in enumerate((bq, bv, bo, g1, s1, b_out, g2, s2)):
            ref[layer : layer + 1, :] = turned[n : n + 1, 0:6]
        b_in[layer : layer + 1, :] = vectors[0:1, 64:88]


def shape(*dims, kind=BRAIN):
    return jax.ShapeDtypeStruct(dims, kind)


VMEM = pl.BlockSpec(memory_space=pltpu.VMEM)
SMEM = pl.BlockSpec(memory_space=pltpu.SMEM)
HBM = pl.BlockSpec(memory_space=pltpu.HBM)


DW_LIMIT = 24
CHAIN_LIMIT = 63
SCALE = 10**9


def call(kernel, ins, outs, scratch, args, micros, limit=63):
    outs = [o if isinstance(o, tuple) else (o, VMEM) for o in outs]
    return pl.pallas_call(
        kernel,
        in_specs=ins,
        out_specs=[o[1] for o in outs],
        out_shape=[o[0] for o in outs],
        scratch_shapes=scratch,
        compiler_params=pltpu.CompilerParams(vmem_limit_bytes=limit * 2**20),
        cost_estimate=pl.CostEstimate(flops=int(micros * SCALE), bytes_accessed=2**20, transcendentals=0),
    )(*args)


def small_call(kernel, outs, args):
    return call(kernel, [VMEM] * len(args), outs, [], args, 1, 12)


def held(kind, *dims):
    return pltpu.VMEM(dims, kind)


def feed_grads(layer, base, own, got, mine, *after):
    out = shape(CHIPS // 2, C_ROWS, 128)
    buffer = held(BRAIN, CHIPS, C_ROWS, 128)
    both = 2 * ROWS
    parts = call(
        lambda *refs: feed_grad_kernel(layer, base, *refs[:3], *refs[3 + len(after) :]),
        [HBM] * (3 + len(after)),
        [(out, HBM)] * 4,
        [held(BRAIN, both, FF), held(BRAIN, both, HALF), held(BRAIN, both, D), held(BRAIN, both, FF // 2), buffer, buffer,
         pltpu.SemaphoreType.DMA((14,)), pltpu.SemaphoreType.DMA((4,))],
        (own, got, mine, *after),
        6,
        DW_LIMIT,
    )
    return parts[:2], parts[2:]


def attend_grads(layer, base, own, got, mine, vectors, bias, *after):
    out = shape(CHIPS // 2, A_ROWS, 128)
    both = 2 * ROWS
    return call(
        lambda *refs: attend_grad_kernel(layer, base, *refs[:5], *refs[5 + len(after) :]),
        [VMEM] * 2 + [HBM] * (3 + len(after)),
        [(out, HBM)] * 2,
        [held(BRAIN, both, D), held(BRAIN, both, D), held(BRAIN, both, 4 * HALF), held(BRAIN, CHIPS, A_ROWS, 128), held(FLOAT, D, 128),
         pltpu.SemaphoreType.DMA((6,)), pltpu.SemaphoreType.DMA((2,))],
        (vectors, bias, own, got, mine, *after),
        5,
        DW_LIMIT,
    )


def body(inputs, lengths, wq, bq, wk, wv, bv, wo, bo, g1, s1, w_in, b_in, w_out, b_out, g2, s2, cotangent):
    wide = shape(ROWS, D, kind=FLOAT)
    f_mine, a_mine = shape(ROWS, FF // 2 + HALF), shape(ROWS, 4 * HALF)
    far = [wide, wide, shape(ROWS, F_WIDTH), shape(ROWS, REST), f_mine, f_mine, a_mine, a_mine]
    out, flow, f1, rest, f_mine0, f_mine1, a_mine0, a_mine1, vectors, bias = call(
        chain_kernel,
        [SMEM] + [VMEM] * 11 + [HBM] * 6,
        [(s, HBM) for s in far] + [shape(LAYERS, 8, D, kind=FLOAT), shape(LAYERS, 1, FF, kind=FLOAT)],
        [pltpu.VMEM(s.shape, s.dtype) for s in far]
        + [held(BRAIN, LAYERS, ROWS, 3 * D), held(BRAIN, LAYERS, PAIRS, 2 * ROWS, ROWS), held(FLOAT, LAYERS, ROWS, D), held(BRAIN, LAYERS, ROWS, FF)]
        + [held(FLOAT, ROWS, D), held(BRAIN, ROWS, FF), held(BRAIN, ROWS, D), held(BRAIN, ROWS, 4 * D), held(BRAIN, ROWS, D)]
        + [held(BRAIN, LAYERS, D, D)] * 4
        + [held(BRAIN, LAYERS, D, FF), held(BRAIN, LAYERS, FF, D)]
        + [pltpu.SemaphoreType.DMA((24,)), pltpu.SemaphoreType.DMA((10,))],
        (lengths, inputs.reshape(ROWS, D), bq, bv, bo, g1, s1, b_in, b_out, g2, s2, cotangent.reshape(ROWS, D), wq, wk, wv, wo, w_in, w_out),
        30,
        CHAIN_LIMIT,
    )
    f1_got = core_swap(f1)
    f1_got, rest = lax.optimization_barrier((f1_got, rest))
    rest_got = core_swap(rest)
    c1, b1 = feed_grads(1, 0, f1, f1_got, f_mine1)
    a1 = attend_grads(1, A1_AT, rest, rest_got, a_mine1, vectors, bias, c1[0])
    c0, b0 = feed_grads(0, F0_AT, rest, rest_got, f_mine0, a1[0])
    a0 = attend_grads(0, A0_AT, rest, rest_got, a_mine0, vectors, bias, c0[0])
    ends = cube_sums({1: (c1, b1, a1), 0: (c0, b0, a0)}, a0[0])
    ends = ends[0] + ends[1]
    own = shape(LAYERS, OWN_ROWS + 2, 128, kind=FLOAT)
    mine, theirs = small_call(last_kernel, [own, shape(LAYERS, OWN_ROWS + 2, 128)], ends)
    matrix, vector = shape(6, LAYERS, D, kind=FLOAT), shape(LAYERS, 6, kind=FLOAT)
    grads = small_call(
        place_kernel,
        [matrix, vector, matrix, matrix, vector, matrix, vector, vector, vector, shape(6, LAYERS, FF, kind=FLOAT),
                   shape(LAYERS, 24, kind=FLOAT), shape(LAYERS, 24, D, kind=FLOAT), vector, vector, vector],
        (mine, core_swap(theirs)),
    )
    turned = (0, 2, 3, 5, 9)
    grads = [g.swapaxes(0, 1) if n in turned else g for n, g in enumerate(grads)]
    return (out.reshape(inputs.shape), flow.reshape(inputs.shape), *grads)


def solution(mesh):
    rows = P(AXES, None, None)
    in_specs = (rows, P(AXES)) + (P(),) * 15 + (rows,)
    wide, thin = P(None, AXES, None), P(None, AXES)
    out_specs = (rows, rows, wide, thin, wide, wide, thin, wide, thin, thin, thin, wide, thin, wide, thin, thin, thin)
    return jax.shard_map(body, mesh=mesh, in_specs=in_specs, out_specs=out_specs, check_vma=False)
```

```python
import jax
import jax.numpy as jnp
import numpy as np
from jax import lax
from jax.experimental import pallas as pl
from jax.experimental.pallas import tpu as pltpu
from jax.sharding import PartitionSpec as P

PAIRS = 6
LAYERS = 2
ROWS = 160
D = 768
FF = 3072
HALF = 384
EPSILON = 1e-12
FLOAT = jnp.float32
BRAIN = jnp.bfloat16
AXES = ("dp", "seq")
DEVICES = 128
CHIPS = 64


def flip(index, dim):
    core, y, x, z = index & 1, (index >> 1) & 3, (index >> 3) & 3, (index >> 5) & 3
    other = lambda i: i ^ 1 if dim < 3 else 3 - i
    if dim % 3 == 0:
        x = other(x)
    elif dim % 3 == 1:
        y = other(y)
    else:
        z = other(z)
    return z * 32 + x * 8 + y * 2 + core


def bit_of(chip, dim):
    coordinate = ((chip >> 2) & 3, chip & 3, chip >> 4)[dim % 3]
    return ((coordinate ^ (coordinate >> 1)) >> (dim // 3)) & 1


SHIFT = (1, 0)


def dim_at(part, step, core):
    layer, part = divmod(part, 3)
    return (part + step + SHIFT[layer]) % 3 + 3 * core if step < 3 else (step + layer) % 3 + 3 * (1 - core)


def slot_base(part, core, chip):
    return sum(bit_of(chip, dim_at(part, step, core)) << (5 - step) for step in range(6))


def own_place():
    index = lax.axis_index(AXES[0]) * 8 + lax.axis_index(AXES[1])
    return index // 2, index % 2


def slots_of(part):
    chip, core = own_place()
    own = jnp.where(core == 0, slot_base(part, 0, chip), slot_base(part, 1, chip))
    return lambda other: jnp.where(core == 0, slot_base(part, 0, other), slot_base(part, 1, other)) ^ own


def cube_send(values, part, *steps):
    pairs = []
    for start in range(DEVICES):
        end = start
        for step in steps:
            end = flip(end, dim_at(part, step, start & 1))
        pairs.append((start, end))
    return lax.ppermute(values, AXES, pairs)


def core_swap(values):
    return lax.ppermute(values, AXES, [(i, i ^ 1) for i in range(DEVICES)])


def add_low(left, right):
    return (left.astype(FLOAT) + right.astype(FLOAT)).astype(BRAIN)


def split_sum(keep, got):
    half = keep.shape[0] // 2
    return add_low(keep[:half], got[:half]), add_low(keep[half:], got[half:])


ORDER = ((2, 0, 1), (0, 1, 2))


class Turns:
    def __init__(self, last):
        self.last = last

    def sum(self, keep, got):
        got, _ = lax.optimization_barrier((got, self.last))
        keep, send = split_sum(keep, got)
        self.last = send
        return keep, send

    def merge(self, parts):
        keeps, gots = [p[0] for p in parts], [p[1] for p in parts]
        gots, _ = lax.optimization_barrier((gots, self.last))
        quarters = merge(*[pair for pair in zip(keeps, gots)])
        self.last = quarters[3]
        return quarters

    def sum_four(self, keep, gots):
        gots, _ = lax.optimization_barrier((gots, self.last))
        whole = sum([got.astype(FLOAT) for got in gots], keep.astype(FLOAT)).astype(BRAIN)
        keep, send = whole[:1], whole[1:]
        self.last = send
        return keep, send


def cube_sums(parts, last):
    turns = Turns(last)
    sent = {}
    for layer in (1, 0):
        sent[layer] = [[keep, cube_send(send, 3 * layer + n, 0)] for n, (send, keep) in enumerate(parts[layer])]
    for step in (1, 2):
        for layer in (1, 0):
            for n in ORDER[layer]:
                keep, send = turns.sum(*sent[layer][n])
                sent[layer][n] = [keep, cube_send(send, 3 * layer + n, step)]
    for layer in (1, 0):
        c, b, a = sent[layer]
        quarters = turns.merge((a, b, c))
        across = ((4,), (3,), (3, 4))
        sent[layer] = [quarters[0], [cube_send(q, 3 * layer, *steps) for q, steps in zip(quarters[1:], across)]]
    for layer in (1, 0):
        keep, send = turns.sum_four(*sent[layer])
        sent[layer] = [keep, cube_send(send, 3 * layer, 5)]
    return sent


def dot(left, right):
    return lax.dot_general(left, right, (((1,), (0,)), ((), ())), preferred_element_type=FLOAT)


def dot_right(left, right):
    return lax.dot_general(left, right, (((1,), (1,)), ((), ())), preferred_element_type=FLOAT)


def dot_left(left, right):
    return lax.dot_general(left, right, (((0,), (0,)), ((), ())), preferred_element_type=FLOAT)


def centred(values):
    centre = values - jnp.mean(values, axis=-1, keepdims=True)
    inverse = lax.rsqrt(jnp.mean(centre * centre, axis=-1, keepdims=True) + EPSILON)
    return centre * inverse, inverse


def norm_back(grad, normal, inverse, gain):
    scaled = grad * gain
    back = scaled - jnp.mean(scaled, axis=-1, keepdims=True)
    back = back - normal * jnp.mean(scaled * normal, axis=-1, keepdims=True)
    return back * inverse, total(grad * normal), total(grad)


def total(values):
    return jnp.sum(values.astype(FLOAT), axis=0, keepdims=True)


def row(ref, layer):
    return ref[layer : layer + 1, :].astype(FLOAT)


def gelu_pair(values):
    cdf = 0.5 + 0.5 * lax.erf(values * np.float32(0.5**0.5))
    density = jnp.exp(-0.5 * values * values) * np.float32((2 * np.pi) ** -0.5)
    return values * cdf, cdf + values * density


def live_of(length, shape, axis):
    return lax.broadcasted_iota(jnp.int32, shape, axis) < length


def two_heads(pair):
    first = lax.broadcasted_iota(jnp.int32, pair.shape, 1) < 64
    none = jnp.zeros_like(pair)
    return jnp.concatenate([jnp.where(first, pair, none), jnp.where(first, none, pair)], axis=0)


def join_heads(both):
    first = lax.broadcasted_iota(jnp.int32, (ROWS, 128), 1) < 64
    return jnp.where(first, both[:ROWS], both[ROWS:])


def half_of(ref, core, width, at=0):
    return ref[:, pl.ds(pl.multiple_of(at + core * width, 128), width)]


F_HID, F_PRE, F_LOW = FF, FF + D, FF + D + FF // 2
F_WIDTH = FF + D + FF // 2 + HALF
A_CTX, A_GRAD = D, 2 * D
A_WIDTH = 2 * D + 4 * HALF
A1_AT, F0_AT, A0_AT = 0, A_WIDTH, A_WIDTH + F_WIDTH
REST = 2 * A_WIDTH + F_WIDTH


class Stream:
    def __init__(self, pairs, sems, ahead):
        self.copies = [pltpu.make_async_copy(source, target, sems.at[n]) for n, (source, target) in enumerate(pairs)]
        self.ahead, self.done, self.begun = ahead, 0, 0
        self.fill()

    def fill(self):
        while self.begun < min(len(self.copies), self.done + self.ahead):
            self.copies[self.begun].start()
            self.begun += 1

    def take(self, count=1):
        for _ in range(count):
            self.copies[self.done].wait()
            self.done += 1
            self.fill()


class Outbox:
    def __init__(self, sems):
        self.sems, self.copies = sems, []

    def send(self, source, target):
        copy = pltpu.make_async_copy(source, target, self.sems.at[len(self.copies)])
        copy.start()
        self.copies.append(copy)

    def finish(self):
        for copy in self.copies:
            copy.wait()


def forward_layer(layer, x, length, small, weights, take, f_ref, a_ref, qkv_ref, probs_ref, mixed_ref, slope_ref):
    bq, bv, bo, g1, s1, b_in, b_out, g2, s2 = small
    wq, wk, wv, wo, w_in, w_out = weights
    rounded = x.astype(BRAIN)
    a_ref[:, :D] = rounded
    take(3)
    qkv_ref[:, 0:D] = ((dot(rounded, wq[layer]) + row(bq, layer)).astype(BRAIN) * 0.125).astype(BRAIN)
    qkv_ref[:, D : 2 * D] = dot(rounded, wk[layer]).astype(BRAIN)
    qkv_ref[:, 2 * D : 3 * D] = (dot(rounded, wv[layer]) + row(bv, layer)).astype(BRAIN)
    keys_live = live_of(length, (2 * ROWS, ROWS), 1)
    lanes = lambda m, pair: slice(m * D + 128 * pair, m * D + 128 * pair + 128)
    scores = [dot_right(two_heads(qkv_ref[:, lanes(0, n)]), qkv_ref[:, lanes(1, n)]) for n in range(PAIRS)]
    for pair in range(PAIRS):
        masked = jnp.where(keys_live, scores[pair], -1e30)
        terms = jnp.exp(masked - jnp.max(masked, axis=-1, keepdims=True))
        probs_ref[pair] = (terms * (1.0 / jnp.sum(terms, axis=-1, keepdims=True))).astype(BRAIN)
    for pair in range(PAIRS):
        context = join_heads(dot(probs_ref[pair], qkv_ref[:, lanes(2, pair)]))
        a_ref[:, A_CTX + 128 * pair : A_CTX + 128 * pair + 128] = context.astype(BRAIN)
    take(1)
    mixed = x + dot(a_ref[:, A_CTX : A_CTX + D], wo[layer]) + row(bo, layer)
    mixed_ref[...] = mixed
    hidden = centred(mixed)[0] * row(g1, layer) + row(s1, layer)
    hidden_low = hidden.astype(BRAIN)
    f_ref[:, F_HID : F_HID + D] = hidden_low
    branch = row(b_out, layer)
    for part in range(4):
        at = slice(part * D, part * D + D)
        take(2)
        pre = dot(hidden_low, w_in[layer, :, at]) + b_in[layer : layer + 1, at].astype(FLOAT)
        act, slope = gelu_pair(pre)
        act = act.astype(BRAIN)
        f_ref[:, at] = act
        slope_ref[:, at] = slope.astype(BRAIN)
        branch = branch + dot(act, w_out[layer, at, :])
    live = live_of(length, (ROWS, 1), 0)
    summed = hidden + jnp.where(live, branch.astype(BRAIN).astype(FLOAT), 0.0)
    normal, inverse = centred(summed)
    result = jnp.where(live, normal * row(g2, layer) + row(s2, layer), 0.0)
    return result, summed, normal, inverse


def feed_back(layer, grad_out, length, core, normal, inverse, g2, wi, wu, slope, g_pre, g_low, mine, f_ref, vectors, bias):
    live = live_of(length, (ROWS, 1), 0)
    grad_live = jnp.where(live, grad_out, 0.0)
    grad_summed, grad_gain, grad_shift = norm_back(grad_live, normal, inverse, row(g2, layer))
    low = jnp.where(live, grad_summed, 0.0).astype(BRAIN)
    g_low[...] = low
    vectors[layer, 5:6, :] = total(low)
    vectors[layer, 6:7, :] = grad_gain
    vectors[layer, 7:8, :] = grad_shift
    back = 0.0
    for part in range(4):
        at = slice(part * D, part * D + D)
        grads = (dot_right(low, wu[at, :]) * slope[:, at].astype(FLOAT)).astype(BRAIN)
        g_pre[:, at] = grads
        bias[layer, :, at] = total(grads)
        back = back + dot_right(grads, wi[:, at])
    for into, side, at in ((mine, core, 0), (f_ref, 1 - core, F_PRE)):
        into[:, at : at + FF // 2] = half_of(g_pre, side, FF // 2)
        into[:, at + FF // 2 : at + FF // 2 + HALF] = half_of(g_low, side, HALF)
    return grad_summed + back.astype(BRAIN).astype(FLOAT)


def attend_back(layer, grad_hidden, core, mixed, g1, qkv, probs, squares, g_all, g_context, mine, a_ref, vectors, ready):
    wq, wk, wv, wo = squares
    normal, inverse = centred(mixed[...])
    grad_mixed, grad_gain, grad_shift = norm_back(grad_hidden, normal, inverse, row(g1, layer))
    low = grad_mixed.astype(BRAIN)
    g_all[:, 3 * D :] = low
    vectors[layer, 2:3, :] = total(low)
    vectors[layer, 3:4, :] = grad_gain
    vectors[layer, 4:5, :] = grad_shift
    g_context[...] = dot_right(low, wo[...]).astype(BRAIN)
    lanes = lambda m, pair: slice(m * D + 128 * pair, m * D + 128 * pair + 128)
    context_two = [two_heads(g_context[:, lanes(0, n)]) for n in range(PAIRS)]
    g_probs = [dot_right(context_two[n], qkv[:, lanes(2, n)]) for n in range(PAIRS)]
    for pair in range(PAIRS):
        g_all[:, lanes(2, pair)] = dot_left(probs[pair], context_two[pair]).astype(BRAIN)
    g_raws = []
    for pair in range(PAIRS):
        weighted = probs[pair].astype(FLOAT)
        weighted_grad = weighted * g_probs[pair]
        g_raws.append((weighted_grad - weighted * jnp.sum(weighted_grad, axis=-1, keepdims=True)).astype(BRAIN))
    for pair in range(PAIRS):
        g_all[:, lanes(0, pair)] = (join_heads(dot(g_raws[pair], qkv[:, lanes(1, pair)])) * 0.125).astype(BRAIN)
    for pair in range(PAIRS):
        g_all[:, lanes(1, pair)] = dot_left(g_raws[pair], two_heads(qkv[:, lanes(0, pair)])).astype(BRAIN)
    g_query, g_keys, g_values = (g_all[:, m * D : m * D + D] for m in range(3))
    vectors[layer, 0:1, :] = total(g_query)
    vectors[layer, 1:2, :] = total(g_values)
    for m in range(4):
        into = m * HALF
        mine[:, into : into + HALF] = half_of(g_all, core, HALF, m * D)
        a_ref[:, A_GRAD + into : A_GRAD + into + HALF] = half_of(g_all, 1 - core, HALF, m * D)
    ready()
    return grad_mixed + dot_right(g_query, wq[...]) + dot_right(g_keys, wk[...]) + dot_right(g_values, wv[...])


AHEAD = 6


def chain_kernel(lengths, x_in, bq, bv, bo, g1, s1, b_in, b_out, g2, s2, cotangent, *refs):
    big, far, refs = refs[:6], refs[6:14], refs[14:]
    vectors, bias, refs = refs[0], refs[1], refs[2:]
    near, refs = refs[:8], refs[8:]
    (qkv, probs, mixed, slope, summed, g_pre, g_low, g_all, g_context), refs = refs[:9], refs[9:]
    weights, (sems, out_sems) = refs[:6], refs[6:]
    out, flow, f1, rest, f_mine0, f_mine1, a_mine0, a_mine1 = near
    a1, f0, a0 = (rest.at[:, at : at + width] for at, width in ((A1_AT, A_WIDTH), (F0_AT, F_WIDTH), (A0_AT, A_WIDTH)))
    length, core = lengths[0], own_place()[1]
    pairs = []
    for layer in range(LAYERS):
        pairs += [(big[n].at[layer], weights[n].at[layer]) for n in range(4)]
        for k in range(4):
            at = slice(k * D, k * D + D)
            pairs.append((big[4].at[layer, :, at], weights[4].at[layer, :, at]))
            pairs.append((big[5].at[layer, at, :], weights[5].at[layer, at, :]))
    stream, outbox = Stream(pairs, sems, AHEAD), Outbox(out_sems)
    small = (bq, bv, bo, g1, s1, b_in, b_out, g2, s2)
    give = lambda *which: [outbox.send(near[n], far[n]) for n in which]
    give_rest = lambda at, width: outbox.send(rest.at[:, at : at + width], far[3].at[:, at : at + width])
    give_a = lambda layer: (give(6 + layer), give_rest(A1_AT if layer == 1 else A0_AT, A_WIDTH))
    give_f = lambda layer: give(2) if layer == 1 else give_rest(F0_AT, F_WIDTH)
    x = x_in[...]
    for layer, (f_ref, a_ref) in enumerate(((f0, a0), (f1, a1))):
        x, total_sum, normal, inverse = forward_layer(layer, x, length, small, weights, stream.take, f_ref, a_ref,
                                                      qkv.at[layer], probs.at[layer], mixed.at[layer], slope.at[layer])
        if layer == 0:
            summed[...] = total_sum
    out[...] = x
    give(0)
    grad = cotangent[...]
    for layer, f_ref, a_ref, f_mine, a_mine in ((1, f1, a1, f_mine1, a_mine1), (0, f0, a0, f_mine0, a_mine0)):
        if layer == 0:
            normal, inverse = centred(summed[...])
        grad = feed_back(layer, grad, length, core, normal, inverse, g2, weights[4].at[layer], weights[5].at[layer], slope.at[layer],
                         g_pre, g_low, f_mine, f_ref, vectors, bias)
        give(4 + layer)
        give_f(layer)
        grad = attend_back(layer, grad, core, mixed.at[layer], g1, qkv.at[layer], probs.at[layer], [w.at[layer] for w in weights[:4]],
                           g_all, g_context, a_mine, a_ref, vectors, lambda layer=layer: give_a(layer))
    flow[...] = grad
    give(1)
    outbox.finish()


def loads(pairs):
    return [(source, target.at[ROWS * n : ROWS * n + ROWS]) for sources, target in pairs for n, source in enumerate(sources)]


def lane_blocks(values):
    return [values[:, 128 * j : 128 * j + 128] for j in range(values.shape[1] // 128)]


def give(outbox, buffer, send, keep):
    outbox.send(buffer.at[CHIPS // 2 :], send)
    outbox.send(buffer.at[: CHIPS // 2], keep)


def feed_grad_kernel(layer, base, own, got, mine, send_c, keep_c, send_b, keep_b,
                     act, low, hidden, pre, buffer_c, buffer_b, sems, out_sems):
    x_of = lambda at, width: tuple(ref.at[:, base + at : base + at + width] for ref in (own, got))
    f_of = lambda at, width: (mine.at[:, at : at + width], got.at[:, base + F_PRE + at : base + F_PRE + at + width])
    pieces = [slice(k * D, k * D + D) for k in range(4)]
    pairs = [(f_of(FF // 2, HALF), low)] + [(x_of(k * D, D), act.at[:, pieces[k]]) for k in range(4)]
    pairs += [(f_of(0, FF // 2), pre), (x_of(F_HID, D), hidden)]
    stream, outbox = Stream(loads(pairs), sems, 14), Outbox(out_sems)
    slot_c, slot_b = slots_of(3 * layer), slots_of(3 * layer + 1)
    stream.take(2)
    for k in range(4):
        stream.take(2)
        grads = dot_left(act[:, pieces[k]], low[...]).astype(BRAIN)
        for n in range(16):
            slot = slot_c(k * 16 + n)
            for j in range(3):
                buffer_c[slot, 48 * j : 48 * j + 48] = grads[48 * n : 48 * n + 48, 128 * j : 128 * j + 128]
    give(outbox, buffer_c, send_c, keep_c)
    stream.take(4)
    for k in range(2):
        blocks = lane_blocks(dot_left(hidden[:, k * HALF : k * HALF + HALF], pre[...]))
        for n in range(32):
            chunk = jnp.concatenate([b[12 * n : 12 * n + 12] for b in blocks], axis=0)
            buffer_b[slot_b(k * 32 + n)] = chunk.astype(BRAIN)
    give(outbox, buffer_b, send_b, keep_b)
    outbox.finish()


def attend_grad_kernel(layer, base, vectors, bias, own, got, mine, send, keep,
                       x_in, context, grads, buffer, turned, sems, out_sems):
    x_of = lambda at, width: tuple(ref.at[:, base + at : base + at + width] for ref in (own, got))
    stream = Stream(loads([((mine, got.at[:, base + A_GRAD : base + A_WIDTH]), grads), (x_of(0, D), x_in), (x_of(A_CTX, D), context)]), sems, 6)
    outbox = Outbox(out_sems)
    slot_a = slots_of(3 * layer + 2)
    turned[...] = jnp.concatenate([vectors[layer], jnp.zeros((120, D), FLOAT)], axis=0).T
    for n in range(DEVICES):
        turned[6 * n : 6 * n + 1, 64:88] = bias[layer, :, 24 * n : 24 * n + 24]
    stream.take(6)
    for k in range(2):
        at = slice(k * HALF, k * HALF + HALF)
        blocks = lane_blocks(dot_left(x_in[:, at], grads[:, : 3 * HALF])) + lane_blocks(dot_left(context[:, at], grads[:, 3 * HALF :]))
        blocks.append(turned[at, :])
        for n in range(32):
            chunk = jnp.concatenate([b[12 * n : 12 * n + 12] for b in blocks] + [jnp.zeros((4, 128), FLOAT)], axis=0)
            buffer[slot_a(k * 32 + n)] = chunk.astype(BRAIN)
    give(outbox, buffer, send, keep)
    outbox.finish()


A_ROWS, B_ROWS, C_ROWS = 160, 144, 144
ALL_ROWS = A_ROWS + B_ROWS + C_ROWS
OWN_ROWS = 25 * 6 + 3 * 24


def merge_kernel(a_keep, a_got, b_keep, b_got, c_keep, c_got, *quarters):
    at = 0
    for rows, mine, got in ((A_ROWS, a_keep, a_got), (B_ROWS, b_keep, b_got), (C_ROWS, c_keep, c_got)):
        summed = (mine[...].astype(FLOAT) + got[...].astype(FLOAT)).astype(BRAIN)
        for n, quarter in enumerate(quarters):
            quarter[:, at : at + rows] = summed[2 * n : 2 * n + 2]
        at += rows


def merge(a, b, c):
    return small_call(merge_kernel, [shape(2, ALL_ROWS, 128)] * 4, (*a, *b, *c))


def last_kernel(keep0, got0, keep1, got1, mine, theirs):
    core = own_place()[1]
    for layer, (keep, got) in enumerate(((keep0, got0), (keep1, got1))):
        summed = keep[0].astype(FLOAT) + got[0].astype(FLOAT)
        low, high = [], []
        starts = [12 * p for p in range(13)] + [A_ROWS + 12 * p for p in range(12)]
        for start in starts:
            low.append(summed[start : start + 6])
            high.append(summed[start + 6 : start + 12])
        for j in range(3):
            start = A_ROWS + B_ROWS + 48 * j
            low.append(summed[start : start + 24])
            high.append(summed[start + 24 : start + 48])
        fill = jnp.zeros((2, 128), FLOAT)
        low, high = jnp.concatenate(low + [fill], axis=0), jnp.concatenate(high + [fill], axis=0)
        mine[layer] = jnp.where(core == 0, low, high)
        theirs[layer] = jnp.where(core == 0, high, low).astype(BRAIN)


def place_kernel(mine, got, wq, bq, wk, wv, bv, wo, bo, g1, s1, w_in, b_in, w_out, b_out, g2, s2):
    core = own_place()[1]
    for layer in range(LAYERS):
        own, other = mine[layer], got[layer].astype(FLOAT)
        sides = (jnp.where(core == 0, own, other), jnp.where(core == 0, other, own))
        for side, rows in enumerate(sides):
            for m, ref in enumerate((wq, wk, wv, wo)):
                for j in range(3):
                    at = 6 * (3 * m + j)
                    ref[:, layer, 384 * side + 128 * j : 384 * side + 128 * j + 128] = rows[at : at + 6]
            for j in range(12):
                at, lane = 6 * (13 + j), 1536 * side + 128 * j
                w_in[:, layer, lane : lane + 128] = rows[at : at + 6]
            for j in range(3):
                at, lane = 150 + 24 * j, 384 * side + 128 * j
                w_out[layer, :, lane : lane + 128] = rows[at : at + 24]
        vectors = own[72:78] + other[72:78]
        turned = jnp.concatenate([vectors, jnp.zeros((122, 128), FLOAT)], axis=0).T
        for n, ref in enumerate((bq, bv, bo, g1, s1, b_out, g2, s2)):
            ref[layer : layer + 1, :] = turned[n : n + 1, 0:6]
        b_in[layer : layer + 1, :] = vectors[0:1, 64:88]


def shape(*dims, kind=BRAIN):
    return jax.ShapeDtypeStruct(dims, kind)


VMEM = pl.BlockSpec(memory_space=pltpu.VMEM)
SMEM = pl.BlockSpec(memory_space=pltpu.SMEM)
HBM = pl.BlockSpec(memory_space=pltpu.HBM)


DW_LIMIT = 24
CHAIN_LIMIT = 63
SCALE = 10**9


def call(kernel, ins, outs, scratch, args, micros, limit=63):
    outs = [o if isinstance(o, tuple) else (o, VMEM) for o in outs]
    return pl.pallas_call(
        kernel,
        in_specs=ins,
        out_specs=[o[1] for o in outs],
        out_shape=[o[0] for o in outs],
        scratch_shapes=scratch,
        compiler_params=pltpu.CompilerParams(vmem_limit_bytes=limit * 2**20),
        cost_estimate=pl.CostEstimate(flops=int(micros * SCALE), bytes_accessed=2**20, transcendentals=0),
    )(*args)


def small_call(kernel, outs, args):
    return call(kernel, [VMEM] * len(args), outs, [], args, 1, 12)


def held(kind, *dims):
    return pltpu.VMEM(dims, kind)


def feed_grads(layer, base, own, got, mine, *after):
    out = shape(CHIPS // 2, C_ROWS, 128)
    buffer = held(BRAIN, CHIPS, C_ROWS, 128)
    both = 2 * ROWS
    parts = call(
        lambda *refs: feed_grad_kernel(layer, base, *refs[:3], *refs[3 + len(after) :]),
        [HBM] * (3 + len(after)),
        [(out, HBM)] * 4,
        [held(BRAIN, both, FF), held(BRAIN, both, HALF), held(BRAIN, both, D), held(BRAIN, both, FF // 2), buffer, buffer,
         pltpu.SemaphoreType.DMA((14,)), pltpu.SemaphoreType.DMA((4,))],
        (own, got, mine, *after),
        6,
        DW_LIMIT,
    )
    return parts[:2], parts[2:]


def attend_grads(layer, base, own, got, mine, vectors, bias, *after):
    out = shape(CHIPS // 2, A_ROWS, 128)
    both = 2 * ROWS
    return call(
        lambda *refs: attend_grad_kernel(layer, base, *refs[:5], *refs[5 + len(after) :]),
        [VMEM] * 2 + [HBM] * (3 + len(after)),
        [(out, HBM)] * 2,
        [held(BRAIN, both, D), held(BRAIN, both, D), held(BRAIN, both, 4 * HALF), held(BRAIN, CHIPS, A_ROWS, 128), held(FLOAT, D, 128),
         pltpu.SemaphoreType.DMA((6,)), pltpu.SemaphoreType.DMA((2,))],
        (vectors, bias, own, got, mine, *after),
        5,
        DW_LIMIT,
    )


def body(inputs, lengths, wq, bq, wk, wv, bv, wo, bo, g1, s1, w_in, b_in, w_out, b_out, g2, s2, cotangent):
    wide = shape(ROWS, D, kind=FLOAT)
    f_mine, a_mine = shape(ROWS, FF // 2 + HALF), shape(ROWS, 4 * HALF)
    far = [wide, wide, shape(ROWS, F_WIDTH), shape(ROWS, REST), f_mine, f_mine, a_mine, a_mine]
    out, flow, f1, rest, f_mine0, f_mine1, a_mine0, a_mine1, vectors, bias = call(
        chain_kernel,
        [SMEM] + [VMEM] * 11 + [HBM] * 6,
        [(s, HBM) for s in far] + [shape(LAYERS, 8, D, kind=FLOAT), shape(LAYERS, 1, FF, kind=FLOAT)],
        [pltpu.VMEM(s.shape, s.dtype) for s in far]
        + [held(BRAIN, LAYERS, ROWS, 3 * D), held(BRAIN, LAYERS, PAIRS, 2 * ROWS, ROWS), held(FLOAT, LAYERS, ROWS, D), held(BRAIN, LAYERS, ROWS, FF)]
        + [held(FLOAT, ROWS, D), held(BRAIN, ROWS, FF), held(BRAIN, ROWS, D), held(BRAIN, ROWS, 4 * D), held(BRAIN, ROWS, D)]
        + [held(BRAIN, LAYERS, D, D)] * 4
        + [held(BRAIN, LAYERS, D, FF), held(BRAIN, LAYERS, FF, D)]
        + [pltpu.SemaphoreType.DMA((24,)), pltpu.SemaphoreType.DMA((10,))],
        (lengths, inputs.reshape(ROWS, D), bq, bv, bo, g1, s1, b_in, b_out, g2, s2, cotangent.reshape(ROWS, D), wq, wk, wv, wo, w_in, w_out),
        30,
        CHAIN_LIMIT,
    )
    f1_got = core_swap(f1)
    f1_got, rest = lax.optimization_barrier((f1_got, rest))
    rest_got = core_swap(rest)
    c1, b1 = feed_grads(1, 0, f1, f1_got, f_mine1)
    a1 = attend_grads(1, A1_AT, rest, rest_got, a_mine1, vectors, bias, c1[0])
    a0 = attend_grads(0, A0_AT, rest, rest_got, a_mine0, vectors, bias, a1[0])
    c0, b0 = feed_grads(0, F0_AT, rest, rest_got, f_mine0, a0[0])
    ends = cube_sums({1: (c1, b1, a1), 0: (c0, b0, a0)}, c0[0])
    ends = ends[0] + ends[1]
    own = shape(LAYERS, OWN_ROWS + 2, 128, kind=FLOAT)
    mine, theirs = small_call(last_kernel, [own, shape(LAYERS, OWN_ROWS + 2, 128)], ends)
    matrix, vector = shape(6, LAYERS, D, kind=FLOAT), shape(LAYERS, 6, kind=FLOAT)
    grads = small_call(
        place_kernel,
        [matrix, vector, matrix, matrix, vector, matrix, vector, vector, vector, shape(6, LAYERS, FF, kind=FLOAT),
                   shape(LAYERS, 24, kind=FLOAT), shape(LAYERS, 24, D, kind=FLOAT), vector, vector, vector],
        (mine, core_swap(theirs)),
    )
    turned = (0, 2, 3, 5, 9)
    grads = [g.swapaxes(0, 1) if n in turned else g for n, g in enumerate(grads)]
    return (out.reshape(inputs.shape), flow.reshape(inputs.shape), *grads)


def solution(mesh):
    rows = P(AXES, None, None)
    in_specs = (rows, P(AXES)) + (P(),) * 15 + (rows,)
    wide, thin = P(None, AXES, None), P(None, AXES)
    out_specs = (rows, rows, wide, thin, wide, wide, thin, wide, thin, thin, thin, wide, thin, wide, thin, thin, thin)
    return jax.shard_map(body, mesh=mesh, in_specs=in_specs, out_specs=out_specs, check_vma=False)
```

```python
import jax
import jax.numpy as jnp
import numpy as np
from jax import lax
from jax.experimental import pallas as pl
from jax.experimental.pallas import tpu as pltpu
from jax.sharding import PartitionSpec as P

PAIRS = 6
LAYERS = 2
ROWS = 160
D = 768
FF = 3072
HALF = 384
EPSILON = 1e-12
FLOAT = jnp.float32
BRAIN = jnp.bfloat16
AXES = ("dp", "seq")
DEVICES = 128
CHIPS = 64


def flip(index, dim):
    core, y, x, z = index & 1, (index >> 1) & 3, (index >> 3) & 3, (index >> 5) & 3
    other = lambda i: i ^ 1 if dim < 3 else 3 - i
    if dim % 3 == 0:
        x = other(x)
    elif dim % 3 == 1:
        y = other(y)
    else:
        z = other(z)
    return z * 32 + x * 8 + y * 2 + core


def bit_of(chip, dim):
    coordinate = ((chip >> 2) & 3, chip & 3, chip >> 4)[dim % 3]
    return ((coordinate ^ (coordinate >> 1)) >> (dim // 3)) & 1


SHIFT = (1, 0)


def dim_at(part, step, core):
    layer, part = divmod(part, 3)
    return (part + step + SHIFT[layer]) % 3 + 3 * core if step < 3 else (step + layer) % 3 + 3 * (1 - core)


def slot_base(part, core, chip):
    return sum(bit_of(chip, dim_at(part, step, core)) << (5 - step) for step in range(6))


def own_place():
    index = lax.axis_index(AXES[0]) * 8 + lax.axis_index(AXES[1])
    return index // 2, index % 2


def slots_of(part):
    chip, core = own_place()
    own = jnp.where(core == 0, slot_base(part, 0, chip), slot_base(part, 1, chip))
    return lambda other: jnp.where(core == 0, slot_base(part, 0, other), slot_base(part, 1, other)) ^ own


def cube_send(values, part, *steps):
    pairs = []
    for start in range(DEVICES):
        end = start
        for step in steps:
            end = flip(end, dim_at(part, step, start & 1))
        pairs.append((start, end))
    return lax.ppermute(values, AXES, pairs)


def core_swap(values):
    return lax.ppermute(values, AXES, [(i, i ^ 1) for i in range(DEVICES)])


def add_low(left, right):
    return (left.astype(FLOAT) + right.astype(FLOAT)).astype(BRAIN)


def split_sum(keep, got):
    half = keep.shape[0] // 2
    return add_low(keep[:half], got[:half]), add_low(keep[half:], got[half:])


ORDER = ((2, 0, 1), (0, 1, 2))


class Turns:
    def __init__(self, last):
        self.last = last

    def sum(self, keep, got):
        got, _ = lax.optimization_barrier((got, self.last))
        keep, send = split_sum(keep, got)
        self.last = send
        return keep, send

    def merge(self, parts):
        keeps, gots = [p[0] for p in parts], [p[1] for p in parts]
        gots, _ = lax.optimization_barrier((gots, self.last))
        quarters = merge(*[pair for pair in zip(keeps, gots)])
        self.last = quarters[3]
        return quarters

    def sum_four(self, keep, gots):
        gots, _ = lax.optimization_barrier((gots, self.last))
        whole = sum([got.astype(FLOAT) for got in gots], keep.astype(FLOAT)).astype(BRAIN)
        keep, send = whole[:1], whole[1:]
        self.last = send
        return keep, send


def cube_sums(parts, last):
    turns = Turns(last)
    sent = {}
    for layer in (1, 0):
        sent[layer] = [[keep, cube_send(send, 3 * layer + n, 0)] for n, (send, keep) in enumerate(parts[layer])]
    for step in (1, 2):
        for layer in (1, 0):
            for n in ORDER[layer]:
                keep, send = turns.sum(*sent[layer][n])
                sent[layer][n] = [keep, cube_send(send, 3 * layer + n, step)]
    for layer in (1, 0):
        c, b, a = sent[layer]
        quarters = turns.merge((a, b, c))
        across = ((4,), (3,), (3, 4))
        sent[layer] = [quarters[0], [cube_send(q, 3 * layer, *steps) for q, steps in zip(quarters[1:], across)]]
    for layer in (1, 0):
        keep, send = turns.sum_four(*sent[layer])
        sent[layer] = [keep, cube_send(send, 3 * layer, 5)]
    return sent


def dot(left, right):
    return lax.dot_general(left, right, (((1,), (0,)), ((), ())), preferred_element_type=FLOAT)


def dot_right(left, right):
    return lax.dot_general(left, right, (((1,), (1,)), ((), ())), preferred_element_type=FLOAT)


def dot_left(left, right):
    return lax.dot_general(left, right, (((0,), (0,)), ((), ())), preferred_element_type=FLOAT)


def centred(values):
    centre = values - jnp.mean(values, axis=-1, keepdims=True)
    inverse = lax.rsqrt(jnp.mean(centre * centre, axis=-1, keepdims=True) + EPSILON)
    return centre * inverse, inverse


def norm_back(grad, normal, inverse, gain):
    scaled = grad * gain
    back = scaled - jnp.mean(scaled, axis=-1, keepdims=True)
    back = back - normal * jnp.mean(scaled * normal, axis=-1, keepdims=True)
    return back * inverse, total(grad * normal), total(grad)


def total(values):
    return jnp.sum(values.astype(FLOAT), axis=0, keepdims=True)


def row(ref, layer):
    return ref[layer : layer + 1, :].astype(FLOAT)


def gelu_pair(values):
    cdf = 0.5 + 0.5 * lax.erf(values * np.float32(0.5**0.5))
    density = jnp.exp(-0.5 * values * values) * np.float32((2 * np.pi) ** -0.5)
    return values * cdf, cdf + values * density


def live_of(length, shape, axis):
    return lax.broadcasted_iota(jnp.int32, shape, axis) < length


def two_heads(pair):
    first = lax.broadcasted_iota(jnp.int32, pair.shape, 1) < 64
    none = jnp.zeros_like(pair)
    return jnp.concatenate([jnp.where(first, pair, none), jnp.where(first, none, pair)], axis=0)


def join_heads(both):
    first = lax.broadcasted_iota(jnp.int32, (ROWS, 128), 1) < 64
    return jnp.where(first, both[:ROWS], both[ROWS:])


def half_of(ref, core, width, at=0):
    return ref[:, pl.ds(pl.multiple_of(at + core * width, 128), width)]


F_HID, F_PRE, F_LOW = FF, FF + D, FF + D + FF // 2
F_WIDTH = FF + D + FF // 2 + HALF
A_CTX, A_GRAD = D, 2 * D
A_WIDTH = 2 * D + 4 * HALF
A1_AT, F0_AT, A0_AT = 0, A_WIDTH, A_WIDTH + F_WIDTH
REST = 2 * A_WIDTH + F_WIDTH


class Stream:
    def __init__(self, pairs, sems, ahead):
        self.copies = [pltpu.make_async_copy(source, target, sems.at[n]) for n, (source, target) in enumerate(pairs)]
        self.ahead, self.done, self.begun = ahead, 0, 0
        self.fill()

    def fill(self):
        while self.begun < min(len(self.copies), self.done + self.ahead):
            self.copies[self.begun].start()
            self.begun += 1

    def take(self, count=1):
        for _ in range(count):
            self.copies[self.done].wait()
            self.done += 1
            self.fill()


class Outbox:
    def __init__(self, sems):
        self.sems, self.copies = sems, []

    def send(self, source, target):
        copy = pltpu.make_async_copy(source, target, self.sems.at[len(self.copies)])
        copy.start()
        self.copies.append(copy)

    def finish(self):
        for copy in self.copies:
            copy.wait()


def forward_layer(layer, x, length, small, weights, take, f_ref, a_ref, qkv_ref, probs_ref, mixed_ref, slope_ref):
    bq, bv, bo, g1, s1, b_in, b_out, g2, s2 = small
    wq, wk, wv, wo, w_in, w_out = weights
    rounded = x.astype(BRAIN)
    a_ref[:, :D] = rounded
    take(3)
    qkv_ref[:, 0:D] = ((dot(rounded, wq[layer]) + row(bq, layer)).astype(BRAIN) * 0.125).astype(BRAIN)
    qkv_ref[:, D : 2 * D] = dot(rounded, wk[layer]).astype(BRAIN)
    qkv_ref[:, 2 * D : 3 * D] = (dot(rounded, wv[layer]) + row(bv, layer)).astype(BRAIN)
    keys_live = live_of(length, (2 * ROWS, ROWS), 1)
    lanes = lambda m, pair: slice(m * D + 128 * pair, m * D + 128 * pair + 128)
    scores = [dot_right(two_heads(qkv_ref[:, lanes(0, n)]), qkv_ref[:, lanes(1, n)]) for n in range(PAIRS)]
    for pair in range(PAIRS):
        masked = jnp.where(keys_live, scores[pair], -1e30)
        terms = jnp.exp(masked - jnp.max(masked, axis=-1, keepdims=True))
        probs_ref[pair] = (terms * (1.0 / jnp.sum(terms, axis=-1, keepdims=True))).astype(BRAIN)
    for pair in range(PAIRS):
        context = join_heads(dot(probs_ref[pair], qkv_ref[:, lanes(2, pair)]))
        a_ref[:, A_CTX + 128 * pair : A_CTX + 128 * pair + 128] = context.astype(BRAIN)
    take(1)
    mixed = x + dot(a_ref[:, A_CTX : A_CTX + D], wo[layer]) + row(bo, layer)
    mixed_ref[...] = mixed
    hidden = centred(mixed)[0] * row(g1, layer) + row(s1, layer)
    hidden_low = hidden.astype(BRAIN)
    f_ref[:, F_HID : F_HID + D] = hidden_low
    branch = row(b_out, layer)
    for part in range(4):
        at = slice(part * D, part * D + D)
        take(2)
        pre = dot(hidden_low, w_in[layer, :, at]) + b_in[layer : layer + 1, at].astype(FLOAT)
        act, slope = gelu_pair(pre)
        act = act.astype(BRAIN)
        f_ref[:, at] = act
        slope_ref[:, at] = slope.astype(BRAIN)
        branch = branch + dot(act, w_out[layer, at, :])
    live = live_of(length, (ROWS, 1), 0)
    summed = hidden + jnp.where(live, branch.astype(BRAIN).astype(FLOAT), 0.0)
    normal, inverse = centred(summed)
    result = jnp.where(live, normal * row(g2, layer) + row(s2, layer), 0.0)
    return result, summed, normal, inverse


def feed_back(layer, grad_out, length, core, normal, inverse, g2, wi, wu, slope, g_pre, g_low, mine, f_ref, vectors, bias):
    live = live_of(length, (ROWS, 1), 0)
    grad_live = jnp.where(live, grad_out, 0.0)
    grad_summed, grad_gain, grad_shift = norm_back(grad_live, normal, inverse, row(g2, layer))
    low = jnp.where(live, grad_summed, 0.0).astype(BRAIN)
    g_low[...] = low
    vectors[layer, 5:6, :] = total(low)
    vectors[layer, 6:7, :] = grad_gain
    vectors[layer, 7:8, :] = grad_shift
    back = 0.0
    for part in range(4):
        at = slice(part * D, part * D + D)
        grads = (dot_right(low, wu[at, :]) * slope[:, at].astype(FLOAT)).astype(BRAIN)
        g_pre[:, at] = grads
        bias[layer, :, at] = total(grads)
        back = back + dot_right(grads, wi[:, at])
    for into, side, at in ((mine, core, 0), (f_ref, 1 - core, F_PRE)):
        into[:, at : at + FF // 2] = half_of(g_pre, side, FF // 2)
        into[:, at + FF // 2 : at + FF // 2 + HALF] = half_of(g_low, side, HALF)
    return grad_summed + back.astype(BRAIN).astype(FLOAT)


def attend_back(layer, grad_hidden, core, mixed, g1, qkv, probs, squares, g_all, g_context, mine, a_ref, vectors, ready):
    wq, wk, wv, wo = squares
    normal, inverse = centred(mixed[...])
    grad_mixed, grad_gain, grad_shift = norm_back(grad_hidden, normal, inverse, row(g1, layer))
    low = grad_mixed.astype(BRAIN)
    g_all[:, 3 * D :] = low
    vectors[layer, 2:3, :] = total(low)
    vectors[layer, 3:4, :] = grad_gain
    vectors[layer, 4:5, :] = grad_shift
    g_context[...] = dot_right(low, wo[...]).astype(BRAIN)
    lanes = lambda m, pair: slice(m * D + 128 * pair, m * D + 128 * pair + 128)
    context_two = [two_heads(g_context[:, lanes(0, n)]) for n in range(PAIRS)]
    g_probs = [dot_right(context_two[n], qkv[:, lanes(2, n)]) for n in range(PAIRS)]
    for pair in range(PAIRS):
        g_all[:, lanes(2, pair)] = dot_left(probs[pair], context_two[pair]).astype(BRAIN)
    g_raws = []
    for pair in range(PAIRS):
        weighted = probs[pair].astype(FLOAT)
        weighted_grad = weighted * g_probs[pair]
        g_raws.append((weighted_grad - weighted * jnp.sum(weighted_grad, axis=-1, keepdims=True)).astype(BRAIN))
    for pair in range(PAIRS):
        g_all[:, lanes(0, pair)] = (join_heads(dot(g_raws[pair], qkv[:, lanes(1, pair)])) * 0.125).astype(BRAIN)
    for pair in range(PAIRS):
        g_all[:, lanes(1, pair)] = dot_left(g_raws[pair], two_heads(qkv[:, lanes(0, pair)])).astype(BRAIN)
    g_query, g_keys, g_values = (g_all[:, m * D : m * D + D] for m in range(3))
    vectors[layer, 0:1, :] = total(g_query)
    vectors[layer, 1:2, :] = total(g_values)
    for m in range(4):
        into = m * HALF
        mine[:, into : into + HALF] = half_of(g_all, core, HALF, m * D)
        a_ref[:, A_GRAD + into : A_GRAD + into + HALF] = half_of(g_all, 1 - core, HALF, m * D)
    ready()
    return grad_mixed + dot_right(g_query, wq[...]) + dot_right(g_keys, wk[...]) + dot_right(g_values, wv[...])


AHEAD = 6


def chain_kernel(lengths, x_in, bq, bv, bo, g1, s1, b_in, b_out, g2, s2, cotangent, *refs):
    big, far, refs = refs[:6], refs[6:15], refs[15:]
    vectors, bias, refs = refs[0], refs[1], refs[2:]
    near, refs = refs[:8], refs[8:]
    (qkv, probs, mixed, slope, summed, g_pre, g_low, g_all, g_context), refs = refs[:9], refs[9:]
    weights, (sems, out_sems) = refs[:6], refs[6:]
    out, flow, f1, rest, f_mine0, f_mine1, a_mine0, a_mine1 = near
    a1, f0, a0 = (rest.at[:, at : at + width] for at, width in ((A1_AT, A_WIDTH), (F0_AT, F_WIDTH), (A0_AT, A_WIDTH)))
    length, core = lengths[0], own_place()[1]
    pairs = []
    for layer in range(LAYERS):
        pairs += [(big[n].at[layer], weights[n].at[layer]) for n in range(4)]
        for k in range(4):
            at = slice(k * D, k * D + D)
            pairs.append((big[4].at[layer, :, at], weights[4].at[layer, :, at]))
            pairs.append((big[5].at[layer, at, :], weights[5].at[layer, at, :]))
    stream, outbox = Stream(pairs, sems, AHEAD), Outbox(out_sems)
    small = (bq, bv, bo, g1, s1, b_in, b_out, g2, s2)
    give = lambda *which: [outbox.send(near[n], far[n]) for n in which]
    give_rest = lambda at, width: outbox.send(rest.at[:, at : at + width], far[3].at[:, at : at + width])
    give_a = lambda layer: (give(6 + layer), give_rest(A1_AT if layer == 1 else A0_AT, A_WIDTH))

    def give_f(layer):
        if layer == 0:
            return give_rest(F0_AT, F_WIDTH)
        outbox.send(f1.at[:, :FF], far[2].at[:, :FF])
        outbox.send(f1.at[:, F_LOW:], far[2].at[:, FF:])
        outbox.send(f1.at[:, F_HID:F_LOW], far[8])

    x = x_in[...]
    for layer, (f_ref, a_ref) in enumerate(((f0, a0), (f1, a1))):
        x, total_sum, normal, inverse = forward_layer(layer, x, length, small, weights, stream.take, f_ref, a_ref,
                                                      qkv.at[layer], probs.at[layer], mixed.at[layer], slope.at[layer])
        if layer == 0:
            summed[...] = total_sum
    out[...] = x
    give(0)
    grad = cotangent[...]
    for layer, f_ref, a_ref, f_mine, a_mine in ((1, f1, a1, f_mine1, a_mine1), (0, f0, a0, f_mine0, a_mine0)):
        if layer == 0:
            normal, inverse = centred(summed[...])
        grad = feed_back(layer, grad, length, core, normal, inverse, g2, weights[4].at[layer], weights[5].at[layer], slope.at[layer],
                         g_pre, g_low, f_mine, f_ref, vectors, bias)
        give(4 + layer)
        give_f(layer)
        grad = attend_back(layer, grad, core, mixed.at[layer], g1, qkv.at[layer], probs.at[layer], [w.at[layer] for w in weights[:4]],
                           g_all, g_context, a_mine, a_ref, vectors, lambda layer=layer: give_a(layer))
    flow[...] = grad
    give(1)
    outbox.finish()


def loads(pairs):
    return [(source, target.at[ROWS * n : ROWS * n + ROWS]) for sources, target in pairs for n, source in enumerate(sources)]


def lane_blocks(values):
    return [values[:, 128 * j : 128 * j + 128] for j in range(values.shape[1] // 128)]


def give(outbox, buffer, send, keep):
    outbox.send(buffer.at[CHIPS // 2 :], send)
    outbox.send(buffer.at[: CHIPS // 2], keep)


def out_grad_kernel(layer, base, own, got, mine, send_c, keep_c, act, low, buffer_c, sems, out_sems):
    x_of = lambda at, width: tuple(ref.at[:, base + at : base + at + width] for ref in (own, got))
    low_of = (mine.at[:, FF // 2 :], got.at[:, FF:])
    pieces = [slice(k * D, k * D + D) for k in range(4)]
    stream = Stream(loads([(low_of, low)] + [(x_of(k * D, D), act.at[:, pieces[k]]) for k in range(4)]), sems, 10)
    outbox = Outbox(out_sems)
    slot_c = slots_of(3 * layer)
    stream.take(2)
    for k in range(4):
        stream.take(2)
        grads = dot_left(act[:, pieces[k]], low[...]).astype(BRAIN)
        for n in range(16):
            slot = slot_c(k * 16 + n)
            for j in range(3):
                buffer_c[slot, 48 * j : 48 * j + 48] = grads[48 * n : 48 * n + 48, 128 * j : 128 * j + 128]
    give(outbox, buffer_c, send_c, keep_c)
    outbox.finish()


def in_grad_kernel(layer, base, own, got, mine, send_b, keep_b, hidden, pre, buffer_b, sems, out_sems):
    x_of = lambda at, width: tuple(ref.at[:, base + at : base + at + width] for ref in (own, got))
    pre_of = (mine.at[:, : FF // 2], got.at[:, base + F_PRE : base + F_LOW])
    stream, outbox = Stream(loads([(pre_of, pre), (x_of(F_HID, D), hidden)]), sems, 4), Outbox(out_sems)
    slot_b = slots_of(3 * layer + 1)
    stream.take(4)
    for k in range(2):
        blocks = lane_blocks(dot_left(hidden[:, k * HALF : k * HALF + HALF], pre[...]))
        for n in range(32):
            chunk = jnp.concatenate([b[12 * n : 12 * n + 12] for b in blocks], axis=0)
            buffer_b[slot_b(k * 32 + n)] = chunk.astype(BRAIN)
    give(outbox, buffer_b, send_b, keep_b)
    outbox.finish()


def feed_grad_kernel(layer, base, own, got, mine, send_c, keep_c, send_b, keep_b,
                     act, low, hidden, pre, buffer_c, buffer_b, sems, out_sems):
    x_of = lambda at, width: tuple(ref.at[:, base + at : base + at + width] for ref in (own, got))
    f_of = lambda at, width: (mine.at[:, at : at + width], got.at[:, base + F_PRE + at : base + F_PRE + at + width])
    pieces = [slice(k * D, k * D + D) for k in range(4)]
    pairs = [(f_of(FF // 2, HALF), low)] + [(x_of(k * D, D), act.at[:, pieces[k]]) for k in range(4)]
    pairs += [(f_of(0, FF // 2), pre), (x_of(F_HID, D), hidden)]
    stream, outbox = Stream(loads(pairs), sems, 14), Outbox(out_sems)
    slot_c, slot_b = slots_of(3 * layer), slots_of(3 * layer + 1)
    stream.take(2)
    for k in range(4):
        stream.take(2)
        grads = dot_left(act[:, pieces[k]], low[...]).astype(BRAIN)
        for n in range(16):
            slot = slot_c(k * 16 + n)
            for j in range(3):
                buffer_c[slot, 48 * j : 48 * j + 48] = grads[48 * n : 48 * n + 48, 128 * j : 128 * j + 128]
    give(outbox, buffer_c, send_c, keep_c)
    stream.take(4)
    for k in range(2):
        blocks = lane_blocks(dot_left(hidden[:, k * HALF : k * HALF + HALF], pre[...]))
        for n in range(32):
            chunk = jnp.concatenate([b[12 * n : 12 * n + 12] for b in blocks], axis=0)
            buffer_b[slot_b(k * 32 + n)] = chunk.astype(BRAIN)
    give(outbox, buffer_b, send_b, keep_b)
    outbox.finish()


def attend_grad_kernel(layer, base, vectors, bias, own, got, mine, send, keep,
                       x_in, context, grads, buffer, turned, sems, out_sems):
    x_of = lambda at, width: tuple(ref.at[:, base + at : base + at + width] for ref in (own, got))
    stream = Stream(loads([((mine, got.at[:, base + A_GRAD : base + A_WIDTH]), grads), (x_of(0, D), x_in), (x_of(A_CTX, D), context)]), sems, 6)
    outbox = Outbox(out_sems)
    slot_a = slots_of(3 * layer + 2)
    turned[...] = jnp.concatenate([vectors[layer], jnp.zeros((120, D), FLOAT)], axis=0).T
    for n in range(DEVICES):
        turned[6 * n : 6 * n + 1, 64:88] = bias[layer, :, 24 * n : 24 * n + 24]
    stream.take(6)
    for k in range(2):
        at = slice(k * HALF, k * HALF + HALF)
        blocks = lane_blocks(dot_left(x_in[:, at], grads[:, : 3 * HALF])) + lane_blocks(dot_left(context[:, at], grads[:, 3 * HALF :]))
        blocks.append(turned[at, :])
        for n in range(32):
            chunk = jnp.concatenate([b[12 * n : 12 * n + 12] for b in blocks] + [jnp.zeros((4, 128), FLOAT)], axis=0)
            buffer[slot_a(k * 32 + n)] = chunk.astype(BRAIN)
    give(outbox, buffer, send, keep)
    outbox.finish()


A_ROWS, B_ROWS, C_ROWS = 160, 144, 144
ALL_ROWS = A_ROWS + B_ROWS + C_ROWS
OWN_ROWS = 25 * 6 + 3 * 24


def merge_kernel(a_keep, a_got, b_keep, b_got, c_keep, c_got, *quarters):
    at = 0
    for rows, mine, got in ((A_ROWS, a_keep, a_got), (B_ROWS, b_keep, b_got), (C_ROWS, c_keep, c_got)):
        summed = (mine[...].astype(FLOAT) + got[...].astype(FLOAT)).astype(BRAIN)
        for n, quarter in enumerate(quarters):
            quarter[:, at : at + rows] = summed[2 * n : 2 * n + 2]
        at += rows


def merge(a, b, c):
    return small_call(merge_kernel, [shape(2, ALL_ROWS, 128)] * 4, (*a, *b, *c))


def last_kernel(keep0, got0, keep1, got1, mine, theirs):
    core = own_place()[1]
    for layer, (keep, got) in enumerate(((keep0, got0), (keep1, got1))):
        summed = keep[0].astype(FLOAT) + got[0].astype(FLOAT)
        low, high = [], []
        starts = [12 * p for p in range(13)] + [A_ROWS + 12 * p for p in range(12)]
        for start in starts:
            low.append(summed[start : start + 6])
            high.append(summed[start + 6 : start + 12])
        for j in range(3):
            start = A_ROWS + B_ROWS + 48 * j
            low.append(summed[start : start + 24])
            high.append(summed[start + 24 : start + 48])
        fill = jnp.zeros((2, 128), FLOAT)
        low, high = jnp.concatenate(low + [fill], axis=0), jnp.concatenate(high + [fill], axis=0)
        mine[layer] = jnp.where(core == 0, low, high)
        theirs[layer] = jnp.where(core == 0, high, low).astype(BRAIN)


def place_kernel(mine, got, wq, bq, wk, wv, bv, wo, bo, g1, s1, w_in, b_in, w_out, b_out, g2, s2):
    core = own_place()[1]
    for layer in range(LAYERS):
        own, other = mine[layer], got[layer].astype(FLOAT)
        sides = (jnp.where(core == 0, own, other), jnp.where(core == 0, other, own))
        for side, rows in enumerate(sides):
            for m, ref in enumerate((wq, wk, wv, wo)):
                for j in range(3):
                    at = 6 * (3 * m + j)
                    ref[:, layer, 384 * side + 128 * j : 384 * side + 128 * j + 128] = rows[at : at + 6]
            for j in range(12):
                at, lane = 6 * (13 + j), 1536 * side + 128 * j
                w_in[:, layer, lane : lane + 128] = rows[at : at + 6]
            for j in range(3):
                at, lane = 150 + 24 * j, 384 * side + 128 * j
                w_out[layer, :, lane : lane + 128] = rows[at : at + 24]
        vectors = own[72:78] + other[72:78]
        turned = jnp.concatenate([vectors, jnp.zeros((122, 128), FLOAT)], axis=0).T
        for n, ref in enumerate((bq, bv, bo, g1, s1, b_out, g2, s2)):
            ref[layer : layer + 1, :] = turned[n : n + 1, 0:6]
        b_in[layer : layer + 1, :] = vectors[0:1, 64:88]


def shape(*dims, kind=BRAIN):
    return jax.ShapeDtypeStruct(dims, kind)


VMEM = pl.BlockSpec(memory_space=pltpu.VMEM)
SMEM = pl.BlockSpec(memory_space=pltpu.SMEM)
HBM = pl.BlockSpec(memory_space=pltpu.HBM)


DW_LIMIT = 24
CHAIN_LIMIT = 63
SCALE = 10**9


def call(kernel, ins, outs, scratch, args, micros, limit=63):
    outs = [o if isinstance(o, tuple) else (o, VMEM) for o in outs]
    return pl.pallas_call(
        kernel,
        in_specs=ins,
        out_specs=[o[1] for o in outs],
        out_shape=[o[0] for o in outs],
        scratch_shapes=scratch,
        compiler_params=pltpu.CompilerParams(vmem_limit_bytes=limit * 2**20),
        cost_estimate=pl.CostEstimate(flops=int(micros * SCALE), bytes_accessed=2**20, transcendentals=0),
    )(*args)


def small_call(kernel, outs, args):
    return call(kernel, [VMEM] * len(args), outs, [], args, 1, 12)


def held(kind, *dims):
    return pltpu.VMEM(dims, kind)


def feed_grads(layer, base, own, got, mine, *after):
    out = shape(CHIPS // 2, C_ROWS, 128)
    buffer = held(BRAIN, CHIPS, C_ROWS, 128)
    both = 2 * ROWS
    parts = call(
        lambda *refs: feed_grad_kernel(layer, base, *refs[:3], *refs[3 + len(after) :]),
        [HBM] * (3 + len(after)),
        [(out, HBM)] * 4,
        [held(BRAIN, both, FF), held(BRAIN, both, HALF), held(BRAIN, both, D), held(BRAIN, both, FF // 2), buffer, buffer,
         pltpu.SemaphoreType.DMA((14,)), pltpu.SemaphoreType.DMA((4,))],
        (own, got, mine, *after),
        6,
        DW_LIMIT,
    )
    return parts[:2], parts[2:]


def feed_grads_apart(layer, c_own, c_got, b_own, b_got, mine):
    out = shape(CHIPS // 2, C_ROWS, 128)
    buffer = held(BRAIN, CHIPS, C_ROWS, 128)
    both = 2 * ROWS
    c = call(
        lambda *refs: out_grad_kernel(layer, 0, *refs),
        [HBM] * 3,
        [(out, HBM)] * 2,
        [held(BRAIN, both, FF), held(BRAIN, both, HALF), buffer, pltpu.SemaphoreType.DMA((10,)), pltpu.SemaphoreType.DMA((2,))],
        (c_own, c_got, mine),
        3,
        DW_LIMIT,
    )
    b = call(
        lambda *refs: in_grad_kernel(layer, -F_HID, *refs[:3], *refs[4:]),
        [HBM] * 4,
        [(out, HBM)] * 2,
        [held(BRAIN, both, D), held(BRAIN, both, FF // 2), buffer, pltpu.SemaphoreType.DMA((4,)), pltpu.SemaphoreType.DMA((2,))],
        (b_own, b_got, mine, c[0]),
        3,
        DW_LIMIT,
    )
    return c, b


def attend_grads(layer, base, own, got, mine, vectors, bias, *after):
    out = shape(CHIPS // 2, A_ROWS, 128)
    both = 2 * ROWS
    return call(
        lambda *refs: attend_grad_kernel(layer, base, *refs[:5], *refs[5 + len(after) :]),
        [VMEM] * 2 + [HBM] * (3 + len(after)),
        [(out, HBM)] * 2,
        [held(BRAIN, both, D), held(BRAIN, both, D), held(BRAIN, both, 4 * HALF), held(BRAIN, CHIPS, A_ROWS, 128), held(FLOAT, D, 128),
         pltpu.SemaphoreType.DMA((6,)), pltpu.SemaphoreType.DMA((2,))],
        (vectors, bias, own, got, mine, *after),
        5,
        DW_LIMIT,
    )


def body(inputs, lengths, wq, bq, wk, wv, bv, wo, bo, g1, s1, w_in, b_in, w_out, b_out, g2, s2, cotangent):
    wide = shape(ROWS, D, kind=FLOAT)
    f_mine, a_mine = shape(ROWS, FF // 2 + HALF), shape(ROWS, 4 * HALF)
    far = [wide, wide, shape(ROWS, F_WIDTH), shape(ROWS, REST), f_mine, f_mine, a_mine, a_mine]
    sent = far[:2] + [shape(ROWS, FF + HALF)] + far[3:] + [shape(ROWS, D + FF // 2)]
    out, flow, c1, rest, f_mine0, f_mine1, a_mine0, a_mine1, b1, vectors, bias = call(
        chain_kernel,
        [SMEM] + [VMEM] * 11 + [HBM] * 6,
        [(s, HBM) for s in sent] + [shape(LAYERS, 8, D, kind=FLOAT), shape(LAYERS, 1, FF, kind=FLOAT)],
        [pltpu.VMEM(s.shape, s.dtype) for s in far]
        + [held(BRAIN, LAYERS, ROWS, 3 * D), held(BRAIN, LAYERS, PAIRS, 2 * ROWS, ROWS), held(FLOAT, LAYERS, ROWS, D), held(BRAIN, LAYERS, ROWS, FF)]
        + [held(FLOAT, ROWS, D), held(BRAIN, ROWS, FF), held(BRAIN, ROWS, D), held(BRAIN, ROWS, 4 * D), held(BRAIN, ROWS, D)]
        + [held(BRAIN, LAYERS, D, D)] * 4
        + [held(BRAIN, LAYERS, D, FF), held(BRAIN, LAYERS, FF, D)]
        + [pltpu.SemaphoreType.DMA((24,)), pltpu.SemaphoreType.DMA((12,))],
        (lengths, inputs.reshape(ROWS, D), bq, bv, bo, g1, s1, b_in, b_out, g2, s2, cotangent.reshape(ROWS, D), wq, wk, wv, wo, w_in, w_out),
        30,
        CHAIN_LIMIT,
    )
    c1_got = core_swap(c1)
    c1_got, b1, rest = lax.optimization_barrier((c1_got, b1, rest))
    c1, b1 = feed_grads_apart(1, c1, c1_got, b1, core_swap(b1), f_mine1)
    rest_got = core_swap(rest)
    a1 = attend_grads(1, A1_AT, rest, rest_got, a_mine1, vectors, bias, b1[0])
    a0 = attend_grads(0, A0_AT, rest, rest_got, a_mine0, vectors, bias, a1[0])
    c0, b0 = feed_grads(0, F0_AT, rest, rest_got, f_mine0, a0[0])
    ends = cube_sums({1: (c1, b1, a1), 0: (c0, b0, a0)}, c0[0])
    ends = ends[0] + ends[1]
    own = shape(LAYERS, OWN_ROWS + 2, 128, kind=FLOAT)
    mine, theirs = small_call(last_kernel, [own, shape(LAYERS, OWN_ROWS + 2, 128)], ends)
    matrix, vector = shape(6, LAYERS, D, kind=FLOAT), shape(LAYERS, 6, kind=FLOAT)
    grads = small_call(
        place_kernel,
        [matrix, vector, matrix, matrix, vector, matrix, vector, vector, vector, shape(6, LAYERS, FF, kind=FLOAT),
                   shape(LAYERS, 24, kind=FLOAT), shape(LAYERS, 24, D, kind=FLOAT), vector, vector, vector],
        (mine, core_swap(theirs)),
    )
    turned = (0, 2, 3, 5, 9)
    grads = [g.swapaxes(0, 1) if n in turned else g for n, g in enumerate(grads)]
    return (out.reshape(inputs.shape), flow.reshape(inputs.shape), *grads)


def solution(mesh):
    rows = P(AXES, None, None)
    in_specs = (rows, P(AXES)) + (P(),) * 15 + (rows,)
    wide, thin = P(None, AXES, None), P(None, AXES)
    out_specs = (rows, rows, wide, thin, wide, wide, thin, wide, thin, thin, thin, wide, thin, wide, thin, thin, thin)
    return jax.shard_map(body, mesh=mesh, in_specs=in_specs, out_specs=out_specs, check_vma=False)
```
